32 devices in a mesh: gx: 4 (over z), gy: 8 (over y, x, core).
Axes of the slice: x: 2, y: 2, z: 4, core: 2. Of those that a mesh axis runs over, the one named last changes fastest.
Arguments:
- flow_state: float32 [4, 32, 64, 128], P(None, 'gx', 'gy'), may hold values from -4.5 to 4.5, as said below
- building_height: int32 [4, 8], P('gx', 'gy'), may hold values from 0 to 8
- pressure_old: float32 [32, 64, 128], P('gx', 'gy'), may hold values from -0.3 to 0.3
Outputs:
- new_state: float32 [4, 32, 64, 128], P(None, 'gx', 'gy')
- pressure: float32 [32, 64, 128], P('gx', 'gy')
The draws below stay inside these ranges and needn't reach their ends.
Inputs may be any that keep to these rules, and one draw needn't show every extreme that they name: `flow_state`: velocity and temperature fluctuations whose size varies across the district.
All inputs are finite; a program needn't handle non-finite values.
Results may differ from the reference program's by a relative error of at most 0.0003.
Values sent between devices are 32-bit elements; how exact they have to be, the bound alone decides.
A program may use at most 64 MiB of HBM per device.

```python
import math
import jax
import jax.numpy as jnp
import numpy as np
from jax import lax

EZ = 16
ITERS = 2
NEX = 4
NEY = 8
NX = 32
NY = 64
NZ = 128


def draw_flow_state(key, part):
    across = (jnp.arange(NX, dtype=jnp.float32) + 0.5) / NX
    along = (jnp.arange(NY, dtype=jnp.float32) + 0.5) / NY
    ramp = (1.0 + 2.0 * across)[:, None] * (1.0 + 2.0 * along)[None, :] / 6.0
    ramp = ramp[None, :, :, None]
    values = jax.random.normal(key, (4, NX, NY, NZ), jnp.float32) * ramp
    return jnp.clip(values, -4.5, 4.5)


def plant(entries, stream_key, least, largest):
    longest = entries.shape.index(max(entries.shape))
    spots = []
    for shift in (0, 1):
        where = [jax.random.randint(jax.random.fold_in(stream_key, axis), (), 0, length) for axis, length in enumerate(entries.shape)]
        where[longest] = (where[longest] + shift) % entries.shape[longest]
        spots.append(tuple(where))
    return entries.at[spots[0]].set(least).at[spots[1]].set(largest)


def steps_of(stream_key, dims, shards, low, largest):
    loudness, own = 1.0, jax.random.fold_in(stream_key, 6)
    for dim, blocks in shards:
        draws = jnp.exp(jax.random.uniform(jax.random.fold_in(own, dim), (blocks,), jnp.float32, low / len(shards), largest / len(shards)))
        loudness = loudness * jnp.repeat(draws, dims[dim] // blocks).reshape([-1 if axis == dim else 1 for axis in range(len(dims))])
    return loudness


def normal_values(stream_key, dims, spread, most, shards=(), kind=jnp.bfloat16):
    drawn = spread * jax.random.normal(stream_key, dims, jnp.float32)
    if shards:
        drawn = drawn * steps_of(stream_key, dims, shards, -0.22, 0.18)
    return jnp.clip(drawn, -most, most).astype(kind)


def setup_inputs(seed: int = 0) -> dict:
    arg_keys = jax.random.split(jax.random.key(seed), 4)
    return {
        "flow_state": draw_flow_state(jax.random.fold_in(arg_keys[3], 71), 0),
        "building_height": plant(jax.random.randint(arg_keys[1], (NEX, NEY), 0, EZ // 2 + 1), jax.random.fold_in(arg_keys[1], 1), 0, (EZ // 2 + 1) - 1).astype(jnp.int32),
        "pressure_old": normal_values(arg_keys[2], (NX, NY, NZ), 0.05, 0.3, ((0, 4), (1, 8)), jnp.float32),
    }


HIGHEST = lax.Precision.HIGHEST
viscosity = 0.05
time_step = 0.01
drag_strength = 20.0
heating = 40.0
buoyancy = 10.0
helmholtz_shift = 0.001
local_shift = 0.5
coarse_shift = 0.02
gll_points = (-1.0, -0.8717401485096066, -0.5917001814331423, -0.2092992179024789, 0.2092992179024789, 0.5917001814331423, 0.8717401485096066, 1.0)

def legendre_seven(points):
    squared = points * points
    return points * (((429.0 * squared - 693.0) * squared + 315.0) * squared - 35.0) / 16.0

def jacobi_eigen(matrix):
    current = np.array(matrix)
    basis = np.eye(8)
    for rounds in range(12):
        for first in range(7):
            for second in range(first + 1, 8):
                rotation_angle = 0.5 * math.atan2(2.0 * float(current[first, second]), float(current[second, second] - current[first, first]))
                cosine = math.cos(rotation_angle)
                sine = math.sin(rotation_angle)
                rotation = np.eye(8)
                rotation[first, first] = cosine
                rotation[second, second] = cosine
                rotation[first, second] = sine
                rotation[second, first] = -sine
                current = rotation.T @ current @ rotation
                basis = basis @ rotation
    return (np.sum(current * np.eye(8), axis=0), basis)

def gll_tables():
    gll_nodes = np.array(gll_points)
    values = legendre_seven(gll_nodes)
    weights = 2.0 / (56.0 * values * values)
    differ = gll_nodes[:, None] - gll_nodes[None, :] + np.eye(8)
    derivative = values[:, None] / values[None, :] / differ * (1.0 - np.eye(8))
    derivative = derivative + np.eye(8) * np.array([-14.0, 0.0, 0.0, 0.0, 0.0, 0.0, 0.0, 14.0])[None, :]
    stiffness = derivative.T @ (weights[:, None] * derivative)
    scaled = stiffness / np.sqrt(np.outer(weights, weights))
    scaled = 0.5 * (scaled + scaled.T)
    eigen_values, eigen_vectors = jacobi_eigen(scaled)
    eigen_basis = eigen_vectors / np.sqrt(weights)[:, None]
    return (gll_nodes, weights, derivative, eigen_basis, np.maximum(eigen_values, 0.0))

def tables():
    return tuple((jnp.asarray(table, dtype=jnp.float32) for table in gll_tables()))

def along_x(field, matrix):
    first, second, third, fourth = field.shape
    blocks = field.reshape(first, second // 8, 8, third, fourth)
    return jnp.einsum('ij,cejyz->ceiyz', matrix, blocks, precision=HIGHEST).reshape(field.shape)

def along_y(field, matrix):
    first, second, third, fourth = field.shape
    blocks = field.reshape(first, second, third // 8, 8, fourth)
    return jnp.einsum('ij,cxejz->cxeiz', matrix, blocks, precision=HIGHEST).reshape(field.shape)

def along_z(field, matrix):
    first, second, third, fourth = field.shape
    blocks = field.reshape(first, second, third, fourth // 8, 8)
    return jnp.einsum('ij,cxyej->cxyei', matrix, blocks, precision=HIGHEST).reshape(field.shape)

def weight_grid(weights, width, depth, height):
    return jnp.tile(weights, width // 8)[:, None, None] * jnp.tile(weights, depth // 8)[None, :, None] * jnp.tile(weights, height // 8)[None, None, :]

def face_counts(count):
    index = jnp.arange(count, dtype=jnp.int32) % 8
    return jnp.where((index == 0) | (index == 7), 2.0, 1.0).astype(jnp.float32)

def multiplicity(width, depth, height):
    vertical_index = jnp.arange(height, dtype=jnp.int32)
    ends = (vertical_index == 0) | (vertical_index == height - 1)
    vertical = jnp.where(ends, 1.0, face_counts(height)).astype(jnp.float32)
    return face_counts(width)[:, None, None] * face_counts(depth)[None, :, None] * vertical[None, None, :]

def canopy_mask(building_height, height):
    column = jnp.repeat(jnp.repeat(building_height, 8, axis=0), 8, axis=1)
    layer = jnp.arange(height, dtype=jnp.int32) // 8
    return (layer[None, None, :] < column[:, :, None]).astype(jnp.float32)

def stiffness_action(field, mass, derivative):
    term = along_x(mass * along_x(field, derivative), derivative.T)
    term = term + along_y(mass * along_y(field, derivative), derivative.T)
    return term + along_z(mass * along_z(field, derivative), derivative.T)

def pair_z(field):
    first, second, third, fourth = field.shape
    blocks = field.reshape(first, second, third, fourth // 8, 8)
    sums = blocks[..., :-1, 7] + blocks[..., 1:, 0]
    starts = jnp.concatenate([blocks[..., :1, 0], sums], axis=3)
    finals = jnp.concatenate([sums, blocks[..., -1:, 7]], axis=3)
    return jnp.concatenate([starts[..., None], blocks[..., 1:7], finals[..., None]], axis=4).reshape(field.shape)

def pair_x(field):
    first, second, third, fourth = field.shape
    blocks = field.reshape(first, second // 8, 8, third, fourth)
    sums = blocks[:, :, 7] + jnp.roll(blocks[:, :, 0], -1, axis=1)
    return jnp.concatenate([jnp.roll(sums, 1, axis=1)[:, :, None], blocks[:, :, 1:7], sums[:, :, None]], axis=2).reshape(field.shape)

def pair_y(field):
    first, second, third, fourth = field.shape
    blocks = field.reshape(first, second, third // 8, 8, fourth)
    sums = blocks[:, :, :, 7] + jnp.roll(blocks[:, :, :, 0], -1, axis=2)
    return jnp.concatenate([jnp.roll(sums, 1, axis=2)[:, :, :, None], blocks[:, :, :, 1:7], sums[:, :, :, None]], axis=3).reshape(field.shape)

def assemble_global(field):
    return pair_z(pair_y(pair_x(field)))

def local_solve(field, eigen_basis, eigen_values):
    first, width, depth, height = field.shape
    spectrum = jnp.tile(eigen_values, width // 8)[:, None, None] + jnp.tile(eigen_values, depth // 8)[None, :, None] + jnp.tile(eigen_values, height // 8)[None, None, :]
    inverse = eigen_basis.T
    modal = along_z(along_y(along_x(field, inverse), inverse), inverse)
    modal = modal / (spectrum + local_shift)
    return along_z(along_y(along_x(modal, eigen_basis), eigen_basis), eigen_basis)

def interpolation(width, periodic, gll_nodes):
    count = width // 8
    columns = count if periodic else count + 1
    position = jnp.tile(gll_nodes, count)
    element = jnp.arange(width, dtype=jnp.int32) // 8
    following = (element + 1) % columns if periodic else element + 1
    target = jnp.arange(columns, dtype=jnp.int32)[None, :]
    left = jnp.where(target == element[:, None], (1.0 - position)[:, None] / 2.0, 0.0)
    right = jnp.where(target == following[:, None], (1.0 + position)[:, None] / 2.0, 0.0)
    return (left + right).astype(jnp.float32)

def restrict(field, across, along, vertical):
    reduced = jnp.einsum('xa,xyz->ayz', across, field, precision=HIGHEST)
    reduced = jnp.einsum('yb,ayz->abz', along, reduced, precision=HIGHEST)
    return jnp.einsum('zc,abz->abc', vertical, reduced, precision=HIGHEST)

def prolong(coarse, across, along, vertical):
    fine = jnp.einsum('zc,abc->abz', vertical, coarse, precision=HIGHEST)
    fine = jnp.einsum('yb,abz->ayz', along, fine, precision=HIGHEST)
    return jnp.einsum('xa,ayz->xyz', across, fine, precision=HIGHEST)

def spectral_tables(count):
    index = jnp.arange(count, dtype=jnp.int32)
    angle = 2.0 * np.pi / count * (index[:, None] * index[None, :] % count).astype(jnp.float32)
    hartley = (jnp.cos(angle) + jnp.sin(angle)) / np.sqrt(count)
    eigen = 2.0 - 2.0 * jnp.cos(2.0 * np.pi / count * index.astype(jnp.float32))
    return (hartley.astype(jnp.float32), eigen.astype(jnp.float32))

def cosine_tables(count):
    index = jnp.arange(count, dtype=jnp.int32).astype(jnp.float32)
    angle = np.pi / count * (index[:, None] + 0.5) * index[None, :]
    norms = jnp.where(index == 0, np.sqrt(1.0 / count), np.sqrt(2.0 / count))
    basis = jnp.cos(angle) * norms[None, :]
    eigen = 2.0 - 2.0 * jnp.cos(np.pi / count * index)
    return (basis.astype(jnp.float32), eigen.astype(jnp.float32))

def coarse_solve(grid):
    first, second, third = grid.shape
    hartley_x, eigen_x = spectral_tables(first)
    hartley_y, eigen_y = spectral_tables(second)
    cosine_z, eigen_z = cosine_tables(third)
    modes = jnp.einsum('ai,ijk->ajk', hartley_x, grid, precision=HIGHEST)
    modes = jnp.einsum('bj,ajk->abk', hartley_y, modes, precision=HIGHEST)
    modes = jnp.einsum('kc,abk->abc', cosine_z, modes, precision=HIGHEST)
    modes = modes / (2.0 * (eigen_x[:, None, None] + eigen_y[None, :, None] + eigen_z[None, None, :]) + coarse_shift)
    values = jnp.einsum('kc,abc->abk', cosine_z, modes, precision=HIGHEST)
    values = jnp.einsum('bj,ajk->abk', hartley_y, values, precision=HIGHEST)
    return jnp.einsum('ai,ijk->ajk', hartley_x, values, precision=HIGHEST)

def provisional_state(flow_state, mass, counts, canopy, derivative, assemble):
    speed = jnp.sqrt(flow_state[0] * flow_state[0] + flow_state[1] * flow_state[1] + flow_state[2] * flow_state[2])
    drag = drag_strength * canopy * speed
    forcing = jnp.stack([-drag * flow_state[0], -drag * flow_state[1], -drag * flow_state[2] + buoyancy * flow_state[3], heating * canopy])
    advection = -(flow_state[0] * along_x(flow_state, derivative) + flow_state[1] * along_y(flow_state, derivative) + flow_state[2] * along_z(flow_state, derivative))
    rate = mass * (advection + forcing) - viscosity * stiffness_action(flow_state, mass, derivative)
    updated = flow_state + time_step * assemble(rate) / (mass * counts)
    height = flow_state.shape[3]
    vertical_index = jnp.arange(height, dtype=jnp.int32)
    wall = jnp.where((vertical_index == 0) | (vertical_index == height - 1), 0.0, 1.0).astype(jnp.float32)
    return jnp.concatenate([updated[:2], updated[2:3] * wall, updated[3:]], axis=0)

def pressure_source(provisional, mass, derivative, assemble):
    divergence = along_x(provisional[0:1], derivative) + along_y(provisional[1:2], derivative) + along_z(provisional[2:3], derivative)
    return -assemble(mass * divergence)

def apply_operator(field, mass, derivative, assemble):
    return assemble(stiffness_action(field, mass, derivative) + helmholtz_shift * mass * field)

def corrected_state(provisional, pressure, mass, counts, derivative, assemble):
    gradient = jnp.concatenate([along_x(pressure, derivative), along_y(pressure, derivative), along_z(pressure, derivative)], axis=0)
    velocity = provisional[:3] - assemble(mass * gradient) / (mass * counts)
    return jnp.concatenate([velocity, provisional[3:]], axis=0)

def inner_sum(first, second, counts):
    return jnp.sum(first * second / counts)

def reference(flow_state, building_height, pressure_old):
    gll_nodes, weights, derivative, eigen_basis, eigen_values = tables()
    first, width, depth, height = flow_state.shape
    mass = weight_grid(weights, width, depth, height)
    counts = multiplicity(width, depth, height)
    canopy = canopy_mask(building_height, height)
    across = interpolation(width, True, gll_nodes)
    along = interpolation(depth, True, gll_nodes)
    vertical = interpolation(height, False, gll_nodes)
    provisional = provisional_state(flow_state, mass, counts, canopy, derivative, assemble_global)
    source = pressure_source(provisional, mass, derivative, assemble_global)

    def operate(field):
        return apply_operator(field, mass, derivative, assemble_global)

    def smooth(residual):
        local = assemble_global(local_solve(residual, eigen_basis, eigen_values))
        coarse = prolong(coarse_solve(restrict(residual[0] / counts, across, along, vertical)), across, along, vertical)
        return local + coarse[None]
    pressure = pressure_old[None]
    residual = source - operate(pressure)
    smoothed = smooth(residual)
    direction = smoothed
    product = inner_sum(residual, smoothed, counts)
    for turn in range(ITERS):
        image = operate(direction)
        alpha = product / inner_sum(direction, image, counts)
        pressure = pressure + alpha * direction
        if turn + 1 < ITERS:
            residual = residual - alpha * image
            smoothed = smooth(residual)
            following = inner_sum(residual, smoothed, counts)
            direction = smoothed + following / product * direction
            product = following
    new_state = corrected_state(provisional, pressure, mass, counts, derivative, assemble_global)
    return (new_state, pressure[0])
```

```python
import functools
import math

import jax
import jax.numpy as jnp
import ml_dtypes
import numpy as np
from jax import lax
from jax.experimental import pallas as pl
from jax.experimental.pallas import tpu as pltpu
from jax.sharding import PartitionSpec as P

F32 = jnp.float32
BF16 = jnp.bfloat16
MESH = pl.DeviceIdType.MESH
N = 8
viscosity = 0.05
time_step = 0.01
drag_strength = 20.0
heating = 40.0
buoyancy = 10.0
helmholtz_shift = 0.001
local_shift = 0.5
coarse_shift = 0.02
gll_points = (
    -1.0,
    -0.8717401485096066,
    -0.5917001814331423,
    -0.2092992179024789,
    0.2092992179024789,
    0.5917001814331423,
    0.8717401485096066,
    1.0,
)


def legendre_seven(points):
    squared = points * points
    return points * (((429.0 * squared - 693.0) * squared + 315.0) * squared - 35.0) / 16.0


def jacobi_eigen(matrix):
    current = np.array(matrix)
    basis = np.eye(8)
    for rounds in range(12):
        for first in range(7):
            for second in range(first + 1, 8):
                rotation_angle = 0.5 * math.atan2(
                    2.0 * float(current[first, second]),
                    float(current[second, second] - current[first, first]),
                )
                cosine = math.cos(rotation_angle)
                sine = math.sin(rotation_angle)
                rotation = np.eye(8)
                rotation[first, first] = cosine
                rotation[second, second] = cosine
                rotation[first, second] = sine
                rotation[second, first] = -sine
                current = rotation.T @ current @ rotation
                basis = basis @ rotation
    return (np.sum(current * np.eye(8), axis=0), basis)


def gll_tables():
    gll_nodes = np.array(gll_points)
    values = legendre_seven(gll_nodes)
    weights = 2.0 / (56.0 * values * values)
    differ = gll_nodes[:, None] - gll_nodes[None, :] + np.eye(8)
    derivative = values[:, None] / values[None, :] / differ * (1.0 - np.eye(8))
    derivative = (
        derivative + np.eye(8) * np.array([-14.0, 0.0, 0.0, 0.0, 0.0, 0.0, 0.0, 14.0])[None, :]
    )
    stiffness = derivative.T @ (weights[:, None] * derivative)
    scaled = stiffness / np.sqrt(np.outer(weights, weights))
    scaled = 0.5 * (scaled + scaled.T)
    eigen_values, eigen_vectors = jacobi_eigen(scaled)
    eigen_basis = eigen_vectors / np.sqrt(weights)[:, None]
    return (gll_nodes, weights, derivative, eigen_basis, np.maximum(eigen_values, 0.0))


def hartley_tables(count):
    index = np.arange(count)
    angle = 2.0 * np.pi / count * (index[:, None] * index[None, :] % count)
    hartley = (np.cos(angle) + np.sin(angle)) / np.sqrt(count)
    return hartley, 2.0 - 2.0 * np.cos(2.0 * np.pi / count * index)


def cosine_tables(count):
    index = np.arange(count)
    angle = np.pi / count * (index[:, None] + 0.5) * index[None, :]
    norms = np.where(index == 0, np.sqrt(1.0 / count), np.sqrt(2.0 / count))
    return np.cos(angle) * norms[None, :], 2.0 - 2.0 * np.cos(np.pi / count * index)


def thirds(matrix):
    pieces = []
    for piece in range(3):
        pieces.append(matrix.astype(np.float32).astype(ml_dtypes.bfloat16))
        matrix = matrix - pieces[-1].astype(np.float64)
    return pieces


def mode_pieces(modes):
    return modes // 128 if modes > 128 and modes % 128 == 0 else 1


DX, DY, KXY = range(3)
ZD, ZK, ZRESTRICT = range(3)
FORWARD, BACK = range(2)
ZFORWARD, ZBACK, ZPROLONG = range(3)
MASS, WXY, WZ, STEP, INVERSE, COPIES, SPECTRUM, CORNERS, SIDES = range(9)


@functools.lru_cache(maxsize=None)
def constants(parts_x, parts_y, height):
    nodes, weights, derivative, basis, values = gll_tables()
    layers = height // N
    levels = layers + 1
    group = height // 4
    assert levels <= group
    eye = np.eye(N)
    diagonal = np.diag(weights)
    stiffness = derivative.T @ diagonal @ derivative

    lefts = np.concatenate(
        [
            np.kron(derivative, eye),
            np.kron(eye, derivative),
            np.kron(stiffness, diagonal) + np.kron(diagonal, stiffness),
        ],
        axis=0,
    )
    high, low, rest = thirds(lefts)
    left_exact = np.concatenate([high, high, low, low, rest], axis=1)
    high, low, rest = thirds(np.concatenate([np.kron(basis.T, basis.T), np.kron(basis, basis)]))
    left_table = np.concatenate([high, high, low, low], axis=1)

    near, far = (1.0 - nodes) / 2.0, (1.0 + nodes) / 2.0
    vertical = np.zeros((height, levels))
    for layer in range(layers):
        vertical[layer * N : layer * N + N, layer] = near
        vertical[layer * N : layer * N + N, layer + 1] = far
    cosine, eigen_z = cosine_tables(levels)
    prolong_z = vertical @ cosine
    place = np.arange(height)
    face = np.where((np.arange(N) == 0) | (np.arange(N) == N - 1), 2.0, 1.0)
    count_z = np.where((place == 0) | (place == height - 1), 1.0, np.tile(face, layers))
    grouped = np.zeros((height, 4, group))
    grouped[:, :, :levels] = prolong_z[:, None, :]
    grouped = grouped.reshape(height, height)
    many = np.eye(layers)
    rights = [np.kron(many, derivative.T), np.kron(many, stiffness)]
    high, low, rest = thirds(np.concatenate(rights, axis=1))
    right_exact = np.concatenate([high, high, low, low, rest], axis=0)
    high, low, rest = thirds(grouped / count_z[:, None])
    right_exact = np.concatenate(
        [right_exact, np.concatenate([high, high, low, low, high], axis=0)], axis=1
    )
    rights = [np.kron(many, basis), np.kron(many, basis.T), grouped.T]
    high, low, rest = thirds(np.concatenate(rights, axis=1))
    right_table = np.concatenate([high, high, low], axis=0)

    weight_xy = np.kron(weights, weights)[:, None] * np.ones((1, height))
    weight_z = np.ones((N * N, 1)) * np.tile(weights, layers)[None, :]
    mass = weight_xy * weight_z
    count_xy = np.kron(face, face)
    copies = count_xy[:, None] * count_z[None, :]
    spectrum = (values[:, None] + values[None, :]).reshape(-1)[:, None] + np.tile(values, layers)
    near_x, far_x = np.repeat(near, N), np.repeat(far, N)
    near_y, far_y = np.tile(near, N), np.tile(far, N)
    sides = np.zeros((N * N, height))
    sides[:, 0], sides[:, 1], sides[:, 2], sides[:, 3] = near_x, far_x, near_y, far_y
    corner = np.stack([near_x * near_y, near_x * far_y, far_x * near_y, far_x * far_y], axis=1)
    corners = np.repeat(corner / count_xy[:, None], group, axis=1)
    plain = np.concatenate(
        [
            mass,
            weight_xy,
            weight_z,
            time_step / (mass * copies),
            1.0 / (mass * copies),
            1.0 / copies,
            1.0 / (spectrum + local_shift),
            corners,
            sides,
        ],
        axis=0,
    ).astype(np.float32)

    hartley_x, eigen_x = hartley_tables(parts_x)
    hartley_y, eigen_y = hartley_tables(parts_y)
    vertex = []
    for step_x in (0, 1):
        for step_y in (0, 1):
            vertex.append(
                np.kron(np.roll(hartley_x, -step_x, axis=1), np.roll(hartley_y, -step_y, axis=1))
            )
    modes = parts_x * parts_y
    pieces = mode_pieces(modes)
    high, low, rest = thirds(np.stack(vertex))
    vertex_table = np.stack([high, low]).reshape(8, pieces, modes // pieces, modes)
    vertex_table = vertex_table.transpose(1, 0, 2, 3).reshape(pieces, -1, modes)
    rows = np.concatenate(
        [np.repeat(hartley_x, parts_y, axis=1), np.tile(hartley_y, (1, parts_x))], axis=0
    ).astype(np.float32)
    rows = rows.reshape(parts_x + parts_y, pieces, -1).transpose(1, 0, 2)
    horizontal = (eigen_x[:, None] + eigen_y[None, :]).reshape(-1)
    inverse = np.zeros((modes, 4, group))
    inverse[:, :, :levels] = (
        1.0 / (2.0 * (horizontal[:, None] + eigen_z[None, :]) + coarse_shift)
    )[:, None, :]
    inverse = inverse.reshape(pieces, -1, height).astype(np.float32)
    return left_exact, right_exact, left_table, right_table, plain, vertex_table, rows, inverse


def split(values):
    high = values.astype(BF16)
    return high, (values - high.astype(F32)).astype(BF16)


def split_thrice(values):
    high = values.astype(BF16)
    rest = values - high.astype(F32)
    low = rest.astype(BF16)
    return high, low, (rest - low.astype(F32)).astype(BF16)


def product(first, second):
    return jnp.dot(first, second, preferred_element_type=F32)


EXCHANGES = (4, 1, 1, 1, 1, 3, 6)
GATHERS = 4


def kernel(
    parts,
    flow_ref,
    roof_ref,
    old_ref,
    left_exact_ref,
    right_exact_ref,
    left_ref,
    right_ref,
    plain_ref,
    vertex_ref,
    rows_ref,
    modes_ref,
    state_ref,
    pressure_ref,
    *scratch,
):
    parts_x, parts_y = parts
    devices = parts_x * parts_y
    count = len(EXCHANGES)
    fields = scratch[0:count]
    y_out = scratch[count : 2 * count]
    c_out = scratch[2 * count : 3 * count]
    x_in = scratch[3 * count : 4 * count]
    y_in = scratch[4 * count : 5 * count]
    c_in = scratch[5 * count : 6 * count]
    row_out, gathered, send_sem, recv_sem, row_send, row_recv = scratch[6 * count :]
    height = old_ref.shape[1]
    points = old_ref.shape[0]

    my_x, my_y = lax.axis_index("gx"), lax.axis_index("gy")
    me = my_x * parts_y + my_y

    barrier = pltpu.get_barrier_semaphore()

    def greet(step, carry):
        other = lax.rem(me + step, devices)
        pl.semaphore_signal(
            barrier, inc=1, device_id=(other // parts_y, lax.rem(other, parts_y)), device_id_type=MESH
        )
        return carry

    lax.fori_loop(1, devices, greet, 0)

    before_x, after_x = lax.rem(my_x + parts_x - 1, parts_x), lax.rem(my_x + 1, parts_x)
    before_y, after_y = lax.rem(my_y + parts_y - 1, parts_y), lax.rem(my_y + 1, parts_y)

    def block(which):
        return plain_ref[which * points : (which + 1) * points, :]

    def left_exact(values, first, last):
        high, low = split(values)
        stacked = jnp.concatenate([high, low, high, low, high], axis=0)
        return product(left_exact_ref[first * points : last * points, :], stacked)

    def right_exact(values, first, last):
        high, low = split(values)
        stacked = jnp.concatenate([high, low, high, low, high], axis=1)
        return product(stacked, right_exact_ref[:, first * height : last * height])

    def left(values, first, last):
        high, low = split(values)
        stacked = jnp.concatenate([high, low, high, low], axis=0)
        return product(left_ref[first * points : last * points, :], stacked)

    def right(values, first, last):
        high, low = split(values)
        stacked = jnp.concatenate([high, low, high], axis=1)
        return product(stacked, right_ref[:, first * height : last * height])

    lane = lax.broadcasted_iota(jnp.int32, (points, height), 1)
    joins_up = (lax.rem(lane, N) == N - 1) & (lane < height - 1)
    joins_down = (lax.rem(lane, N) == 0) & (lane > 0)

    def pair_z(values):
        up = pltpu.roll(values, height - 1, 1)
        down = pltpu.roll(values, 1, 1)
        return values + jnp.where(joins_up, up, jnp.where(joins_down, down, 0.0))

    def copies(which):
        field, number = fields[which], EXCHANGES[which]
        plan = []
        x_faces = (field.at[:, points - N : points, :], field.at[:, 0:N, :])
        for side, target in ((0, after_x), (1, before_x)):
            plan.append((x_faces[side], x_in[which].at[side], (target, my_y)))
        for side, target in ((0, after_y), (1, before_y)):
            plan.append((y_out[which].at[side], y_in[which].at[side], (my_x, target)))
        for corner, target in enumerate(
            ((after_x, after_y), (after_x, before_y), (before_x, after_y), (before_x, before_y))
        ):
            plan.append((c_out[which].at[corner], c_in[which].at[corner], target))
        return [
            pltpu.make_async_remote_copy(
                src_ref=source,
                dst_ref=landing,
                send_sem=send_sem.at[which, index],
                recv_sem=recv_sem.at[which, index],
                device_id=target,
                device_id_type=MESH,
            )
            for index, (source, landing, target) in enumerate(plan)
        ]

    def start(which, values):
        field, number = fields[which], EXCHANGES[which]
        values = [pair_z(value) for value in values]
        for index, value in enumerate(values):
            field[index] = value
            solid = value.reshape(N, N, height)
            y_out[which][0, index * N : index * N + N, :] = solid[:, N - 1, :]
            y_out[which][1, index * N : index * N + N, :] = solid[:, 0, :]
            for corner, row in enumerate((points - 1, points - N, N - 1, 0)):
                c_out[which][corner, index : index + 1, :] = value[row : row + 1, :]
        plan = copies(which)
        for copy in plan:
            copy.start()
        return values

    row_of_x = lax.broadcasted_iota(jnp.int32, (N, height), 0)

    def finish(which, values):
        plan = copies(which)
        for copy in plan:
            copy.wait_recv()
        results = []
        for index, value in enumerate(values):
            solid = value.reshape(N, N, height)
            from_x = x_in[which][:, index]
            first_y = y_in[which][0, index * N : index * N + N, :]
            last_y = y_in[which][1, index * N : index * N + N, :]
            corner = [c_in[which][which_one, index : index + 1, :] for which_one in range(4)]
            first_y = first_y + jnp.where(row_of_x == 0, corner[0], 0.0)
            last_y = last_y + jnp.where(row_of_x == 0, corner[1], 0.0)
            first_y = first_y + jnp.where(row_of_x == N - 1, corner[2], 0.0)
            last_y = last_y + jnp.where(row_of_x == N - 1, corner[3], 0.0)
            slabs = []
            for x in range(N):
                slab = solid[x]
                if x == 0:
                    slab = slab + from_x[0]
                if x == N - 1:
                    slab = slab + from_x[1]
                slab = slab + jnp.where(row_of_x == 0, first_y[x : x + 1, :], 0.0)
                slab = slab + jnp.where(row_of_x == N - 1, last_y[x : x + 1, :], 0.0)
                slabs.append(slab)
            results.append(jnp.concatenate(slabs, axis=0))
        return results

    def spread(which, row):
        row_out[which] = row
        gathered[which, pl.ds(me, 1), :] = row

        def send(step, carry):
            other = lax.rem(me + step, devices)
            pltpu.make_async_remote_copy(
                src_ref=row_out.at[which],
                dst_ref=gathered.at[which, pl.ds(me, 1), :],
                send_sem=row_send.at[which],
                recv_sem=row_recv.at[which],
                device_id=(other // parts_y, lax.rem(other, parts_y)),
                device_id_type=MESH,
            ).start()
            return carry

        lax.fori_loop(1, devices, send, 0)

    def all_rows(which):
        return pltpu.make_async_remote_copy(
            src_ref=gathered.at[which, pl.ds(0, devices - 1), :],
            dst_ref=gathered.at[which, pl.ds(0, devices - 1), :],
            send_sem=row_send.at[which],
            recv_sem=row_recv.at[which],
            device_id=(after_x, my_y),
            device_id_type=MESH,
        )

    def collect(which):
        all_rows(which).wait_recv()
        return gathered[which]

    mass, weight_xy, weight_z = block(MASS), block(WXY), block(WZ)
    one_row = lax.broadcasted_iota(jnp.int32, (1, height), 1)

    def operate(values):
        xy = left_exact(values, DX, KXY + 1)
        z = right_exact(values, ZD, ZK + 1)
        image = xy[2 * points :] * weight_z + weight_xy * z[:, height:]
        gradient = [mass * xy[:points], mass * xy[points : 2 * points], mass * z[:, :height]]
        return image + helmholtz_shift * mass * values, gradient

    def coarse_send(which, residual):
        high, low, rest = split_thrice(residual)
        stacked = jnp.concatenate([high, low, high, low, rest], axis=1)
        table = right_exact_ref[:, ZRESTRICT * height : (ZRESTRICT + 1) * height]
        terms = block(CORNERS) * product(stacked, table)
        spread(which, jnp.sum(terms, axis=0, keepdims=True))

    def local_solve(residual):
        modal = right(left(residual, FORWARD, FORWARD + 1), ZFORWARD, ZFORWARD + 1)
        modal = modal * block(SPECTRUM)
        return left(right(modal, ZBACK, ZBACK + 1), BACK, BACK + 1)

    def own_modes(piece):
        sides = block(SIDES)
        next_x, next_y = lax.rem(my_x + 1, parts_x), lax.rem(my_y + 1, parts_y)

        def row(which):
            return rows_ref[piece, pl.ds(which, 1), :]

        own_x = sides[:, 0:1] * row(my_x) + sides[:, 1:2] * row(next_x)
        own_y = sides[:, 2:3] * row(parts_x + my_y) + sides[:, 3:4] * row(parts_x + next_y)
        return split(own_x * own_y)

    pieces = modes_ref.shape[0]
    length = modes_ref.shape[1]
    span = length if pieces == 1 else 2 * length
    mode_lane = lax.broadcasted_iota(jnp.int32, (length, height), 1)
    group = height // 4

    def coarse_piece(piece, stacked, own):
        each = product(vertex_ref[piece, :, :span], stacked[:span])
        for begin in range(span, devices, span):
            lines = slice(begin, begin + span)
            each = each + product(vertex_ref[piece, :, lines], stacked[lines])
        tops, lows = each[: 4 * length], each[4 * length :]
        each = (tops[:, 2 * height :] + lows[:, height : 2 * height]) + (
            tops[:, height : 2 * height] + lows[:, :height]
        )
        each = each + tops[:, :height]
        total = jnp.zeros((length, height), F32)
        for corner in range(4):
            chosen = (mode_lane >= corner * group) & (mode_lane < corner * group + group)
            total = jnp.where(chosen, each[corner * length : (corner + 1) * length], total)
        levels = right(total * modes_ref[piece], ZPROLONG, ZPROLONG + 1)
        high, low = split(levels)
        own_high, own_low = own
        return product(own_high, high) + (product(own_high, low) + product(own_low, high))

    def coarse_finish(which):
        stacked = jnp.concatenate(split_thrice(collect(which)), axis=1)
        if pieces == 1:
            return coarse_piece(0, stacked, own)
        total = jnp.zeros((points, height), F32)
        for piece in range(pieces):
            total = total + coarse_piece(piece, stacked, own_modes(piece))
        return total

    def scalars_send(which, residual, smoothed, image):
        gamma = jnp.sum(residual * smoothed * block(COPIES), axis=0, keepdims=True)
        delta = jnp.sum(smoothed * image, axis=0, keepdims=True)
        gamma = gamma + pltpu.roll(gamma, height // 2, 1)
        delta = delta + pltpu.roll(delta, height // 2, 1)
        spread(which, jnp.where(one_row < height // 2, gamma, delta))

    def scalars_finish(which):
        total = jnp.sum(collect(which), axis=0, keepdims=True)
        gamma = jnp.sum(jnp.where(one_row < height // 2, total, 0.0), axis=1, keepdims=True)
        delta = jnp.sum(jnp.where(one_row < height // 2, 0.0, total), axis=1, keepdims=True)
        return gamma, delta

    flow = [flow_ref[part * points : (part + 1) * points, :] for part in range(4)]
    u, v, w, theta = flow
    xy = left_exact(jnp.concatenate(flow, axis=1), DX, KXY + 1)
    z = right_exact(flow_ref[...], ZD, ZK + 1)
    canopy = jnp.where(lane // N < roof_ref[0, 0], 1.0, 0.0)
    drag = drag_strength * canopy * jnp.sqrt(u * u + v * v + w * w)
    forcing = [-drag * u, -drag * v, -drag * w + buoyancy * theta, heating * canopy]
    rates = []
    for part in range(4):
        lanes = slice(part * height, (part + 1) * height)
        rows = slice(part * points, (part + 1) * points)
        advection = u * xy[:points, lanes] + v * xy[points : 2 * points, lanes] + w * z[rows, :height]
        friction = xy[2 * points :, lanes] * weight_z + weight_xy * z[rows, height:]
        rates.append(mass * (forcing[part] - advection) - viscosity * friction)
    pl.semaphore_wait(barrier, devices - 1)
    rates = start(0, rates)

    old = old_ref[...]
    old_image, old_gradient = operate(old)
    own = own_modes(0) if pieces == 1 else None

    rates = finish(0, rates)
    step = block(STEP)
    provisional = [values + step * rate for values, rate in zip(flow, rates)]
    provisional[2] = jnp.where((lane == 0) | (lane == height - 1), 0.0, provisional[2])
    divergence = (
        left_exact(provisional[0], DX, DX + 1)
        + left_exact(provisional[1], DY, DY + 1)
        + right_exact(provisional[2], ZD, ZD + 1)
    )
    residual = finish(1, start(1, [-mass * divergence - old_image]))[0]

    coarse_send(0, residual)
    local = start(2, [local_solve(residual)])
    coarse = coarse_finish(0)
    first = finish(2, local)[0] + coarse
    image, first_gradient = operate(first)
    scalars_send(1, residual, first, image)
    image = start(3, [image])
    gradients = start(6, old_gradient + first_gradient)
    gamma_first, delta_first = scalars_finish(1)
    alpha_first = gamma_first / delta_first
    residual = residual - alpha_first * finish(3, image)[0]

    coarse_send(2, residual)
    local = start(4, [local_solve(residual)])
    coarse = coarse_finish(2)
    second = finish(4, local)[0] + coarse
    image, second_gradient = operate(second)
    scalars_send(3, residual, second, image)
    second_gradient = start(5, second_gradient)
    gradients = finish(6, gradients)
    gamma, delta = scalars_finish(3)
    ratio = gamma / gamma_first
    alpha = gamma / (delta - ratio * gamma / alpha_first)
    weight_first = alpha_first + alpha * ratio
    pressure_ref[...] = old + weight_first * first + alpha * second
    state_ref[3 * points : 4 * points, :] = provisional[3]
    second_gradient = finish(5, second_gradient)
    inverse = block(INVERSE)
    for part in range(3):
        total = gradients[part] + weight_first * gradients[3 + part] + alpha * second_gradient[part]
        state_ref[part * points : (part + 1) * points, :] = provisional[part] - total * inverse

    for which in range(count):
        for copy in copies(which):
            copy.wait_send()
    for which in range(GATHERS):
        all_rows(which).wait_send()


def on_device(flow_state, building_height, pressure_old):
    parts = (lax.axis_size("gx"), lax.axis_size("gy"))
    devices = parts[0] * parts[1]
    components, width, depth, height = flow_state.shape
    points = width * depth
    assert width == N and depth == N and components == 4
    tables = constants(parts[0], parts[1], height)
    scratch = [pltpu.VMEM((number, points, height), F32) for number in EXCHANGES]
    scratch += [pltpu.VMEM((2, number * N, height), F32) for number in EXCHANGES]
    scratch += [pltpu.VMEM((4, number, height), F32) for number in EXCHANGES]
    scratch += [pltpu.VMEM((2, number, N, height), F32) for number in EXCHANGES]
    scratch += [pltpu.VMEM((2, number * N, height), F32) for number in EXCHANGES]
    scratch += [pltpu.VMEM((4, number, height), F32) for number in EXCHANGES]
    scratch += [
        pltpu.VMEM((GATHERS, 1, height), F32),
        pltpu.VMEM((GATHERS, devices, height), F32),
        pltpu.SemaphoreType.DMA((len(EXCHANGES), 8)),
        pltpu.SemaphoreType.DMA((len(EXCHANGES), 8)),
        pltpu.SemaphoreType.DMA((GATHERS,)),
        pltpu.SemaphoreType.DMA((GATHERS,)),
    ]
    whole = pl.BlockSpec(memory_space=pltpu.VMEM)
    scalar = pl.BlockSpec(memory_space=pltpu.SMEM)
    state, pressure = pl.pallas_call(
        functools.partial(kernel, parts),
        out_shape=(
            jax.ShapeDtypeStruct((components * points, height), F32),
            jax.ShapeDtypeStruct((points, height), F32),
        ),
        in_specs=[whole, scalar] + [whole] * 9,
        out_specs=(whole, whole),
        scratch_shapes=scratch,
        compiler_params=pltpu.CompilerParams(
            collective_id=0, has_side_effects=True, vmem_limit_bytes=48 * 2**20
        ),
    )(
        flow_state.reshape(components * points, height),
        building_height,
        pressure_old.reshape(points, height),
        *[jnp.asarray(table) for table in tables],
    )
    return state.reshape(flow_state.shape), pressure.reshape(pressure_old.shape)


def solution(mesh):
    in_specs = (P(None, "gx", "gy", None), P("gx", "gy"), P("gx", "gy", None))
    out_specs = (P(None, "gx", "gy", None), P("gx", "gy", None))
    return jax.shard_map(
        on_device, mesh=mesh, in_specs=in_specs, out_specs=out_specs, check_vma=False
    )
```

```python
import functools
import math

import jax
import jax.numpy as jnp
import ml_dtypes
import numpy as np
from jax import lax
from jax.experimental import pallas as pl
from jax.experimental.pallas import tpu as pltpu
from jax.sharding import PartitionSpec as P

F32 = jnp.float32
BF16 = jnp.bfloat16
MESH = pl.DeviceIdType.MESH
N = 8
viscosity = 0.05
time_step = 0.01
drag_strength = 20.0
heating = 40.0
buoyancy = 10.0
helmholtz_shift = 0.001
local_shift = 0.5
coarse_shift = 0.02
gll_points = (
    -1.0,
    -0.8717401485096066,
    -0.5917001814331423,
    -0.2092992179024789,
    0.2092992179024789,
    0.5917001814331423,
    0.8717401485096066,
    1.0,
)


def legendre_seven(points):
    squared = points * points
    return points * (((429.0 * squared - 693.0) * squared + 315.0) * squared - 35.0) / 16.0


def jacobi_eigen(matrix):
    current = np.array(matrix)
    basis = np.eye(8)
    for rounds in range(12):
        for first in range(7):
            for second in range(first + 1, 8):
                rotation_angle = 0.5 * math.atan2(
                    2.0 * float(current[first, second]),
                    float(current[second, second] - current[first, first]),
                )
                cosine = math.cos(rotation_angle)
                sine = math.sin(rotation_angle)
                rotation = np.eye(8)
                rotation[first, first] = cosine
                rotation[second, second] = cosine
                rotation[first, second] = sine
                rotation[second, first] = -sine
                current = rotation.T @ current @ rotation
                basis = basis @ rotation
    return (np.sum(current * np.eye(8), axis=0), basis)


def gll_tables():
    gll_nodes = np.array(gll_points)
    values = legendre_seven(gll_nodes)
    weights = 2.0 / (56.0 * values * values)
    differ = gll_nodes[:, None] - gll_nodes[None, :] + np.eye(8)
    derivative = values[:, None] / values[None, :] / differ * (1.0 - np.eye(8))
    derivative = (
        derivative + np.eye(8) * np.array([-14.0, 0.0, 0.0, 0.0, 0.0, 0.0, 0.0, 14.0])[None, :]
    )
    stiffness = derivative.T @ (weights[:, None] * derivative)
    scaled = stiffness / np.sqrt(np.outer(weights, weights))
    scaled = 0.5 * (scaled + scaled.T)
    eigen_values, eigen_vectors = jacobi_eigen(scaled)
    eigen_basis = eigen_vectors / np.sqrt(weights)[:, None]
    return (gll_nodes, weights, derivative, eigen_basis, np.maximum(eigen_values, 0.0))


def hartley_tables(count):
    index = np.arange(count)
    angle = 2.0 * np.pi / count * (index[:, None] * index[None, :] % count)
    hartley = (np.cos(angle) + np.sin(angle)) / np.sqrt(count)
    return hartley, 2.0 - 2.0 * np.cos(2.0 * np.pi / count * index)


def cosine_tables(count):
    index = np.arange(count)
    angle = np.pi / count * (index[:, None] + 0.5) * index[None, :]
    norms = np.where(index == 0, np.sqrt(1.0 / count), np.sqrt(2.0 / count))
    return np.cos(angle) * norms[None, :], 2.0 - 2.0 * np.cos(np.pi / count * index)


def thirds(matrix):
    pieces = []
    for piece in range(3):
        pieces.append(matrix.astype(np.float32).astype(ml_dtypes.bfloat16))
        matrix = matrix - pieces[-1].astype(np.float64)
    return pieces


def mode_pieces(modes):
    return modes // 128 if modes > 128 and modes % 128 == 0 else 1


DX, DY, KXY = range(3)
ZD, ZK, ZRESTRICT = range(3)
FORWARD, BACK = range(2)
ZFORWARD, ZBACK, ZPROLONG = range(3)
MASS, WXY, WZ, STEP, INVERSE, COPIES, SPECTRUM, CORNERS, SIDES = range(9)


@functools.lru_cache(maxsize=None)
def constants(parts_x, parts_y, height):
    nodes, weights, derivative, basis, values = gll_tables()
    layers = height // N
    levels = layers + 1
    group = height // 4
    assert levels + 2 <= group
    eye = np.eye(N)
    diagonal = np.diag(weights)
    stiffness = derivative.T @ diagonal @ derivative

    lefts = np.concatenate(
        [
            np.kron(derivative, eye),
            np.kron(eye, derivative),
            np.kron(stiffness, diagonal) + np.kron(diagonal, stiffness),
        ],
        axis=0,
    )
    high, low, rest = thirds(lefts)
    left_exact = np.concatenate([high, high, low, low, rest], axis=1)
    high, low, rest = thirds(np.concatenate([np.kron(basis.T, basis.T), np.kron(basis, basis)]))
    left_table = np.concatenate([high, high, low, low], axis=1)

    near, far = (1.0 - nodes) / 2.0, (1.0 + nodes) / 2.0
    vertical = np.zeros((height, levels))
    for layer in range(layers):
        vertical[layer * N : layer * N + N, layer] = near
        vertical[layer * N : layer * N + N, layer + 1] = far
    cosine, eigen_z = cosine_tables(levels)
    prolong_z = vertical @ cosine
    place = np.arange(height)
    face = np.where((np.arange(N) == 0) | (np.arange(N) == N - 1), 2.0, 1.0)
    count_z = np.where((place == 0) | (place == height - 1), 1.0, np.tile(face, layers))
    grouped = np.zeros((height, 4, group))
    grouped[:, :, :levels] = prolong_z[:, None, :]
    grouped = grouped.reshape(height, height)
    many = np.eye(layers)
    rights = [np.kron(many, derivative.T), np.kron(many, stiffness)]
    high, low, rest = thirds(np.concatenate(rights, axis=1))
    right_exact = np.concatenate([high, high, low, low, rest], axis=0)
    high, low, rest = thirds(grouped)
    right_exact = np.concatenate(
        [right_exact, np.concatenate([high, high, low, low, high], axis=0)], axis=1
    )
    rights = [np.kron(many, basis), np.kron(many, basis.T), grouped.T]
    high, low, rest = thirds(np.concatenate(rights, axis=1))
    right_table = np.concatenate([high, high, low], axis=0)

    weight_xy = np.kron(weights, weights)[:, None] * np.ones((1, height))
    weight_z = np.ones((N * N, 1)) * np.tile(weights, layers)[None, :]
    mass = weight_xy * weight_z
    count_xy = np.kron(face, face)
    copies = count_xy[:, None] * count_z[None, :]
    spectrum = (values[:, None] + values[None, :]).reshape(-1)[:, None] + np.tile(values, layers)
    near_x, far_x = np.repeat(near, N), np.repeat(far, N)
    near_y, far_y = np.tile(near, N), np.tile(far, N)
    sides = np.zeros((N * N, height))
    sides[:, 0], sides[:, 1], sides[:, 2], sides[:, 3] = near_x, far_x, near_y, far_y
    corner = np.stack([near_x * near_y, near_x * far_y, far_x * near_y, far_x * far_y], axis=1)
    corners = np.repeat(corner, group, axis=1)
    plain = np.concatenate(
        [
            mass,
            weight_xy,
            weight_z,
            time_step / (mass * copies),
            1.0 / (mass * copies),
            1.0 / copies,
            1.0 / (spectrum + local_shift),
            corners,
            sides,
        ],
        axis=0,
    ).astype(np.float32)

    hartley_x, eigen_x = hartley_tables(parts_x)
    hartley_y, eigen_y = hartley_tables(parts_y)
    vertex = []
    for step_x in (0, 1):
        for step_y in (0, 1):
            vertex.append(
                np.kron(np.roll(hartley_x, -step_x, axis=1), np.roll(hartley_y, -step_y, axis=1))
            )
    modes = parts_x * parts_y
    pieces = mode_pieces(modes)
    high, low, rest = thirds(np.stack(vertex))
    vertex_table = np.stack([high, low]).reshape(8, pieces, modes // pieces, modes)
    vertex_table = vertex_table.transpose(1, 0, 2, 3).reshape(pieces, -1, modes)
    rows = np.concatenate(
        [np.repeat(hartley_x, parts_y, axis=1), np.tile(hartley_y, (1, parts_x))], axis=0
    ).astype(np.float32)
    rows = rows.reshape(parts_x + parts_y, pieces, -1).transpose(1, 0, 2)
    horizontal = (eigen_x[:, None] + eigen_y[None, :]).reshape(-1)
    inverse = np.zeros((modes, 4, group))
    inverse[:, :, :levels] = (
        1.0 / (2.0 * (horizontal[:, None] + eigen_z[None, :]) + coarse_shift)
    )[:, None, :]
    inverse = inverse.reshape(pieces, -1, height).astype(np.float32)
    return left_exact, right_exact, left_table, right_table, plain, vertex_table, rows, inverse


def split(values):
    high = values.astype(BF16)
    return high, (values - high.astype(F32)).astype(BF16)


def split_thrice(values):
    high = values.astype(BF16)
    rest = values - high.astype(F32)
    low = rest.astype(BF16)
    return high, low, (rest - low.astype(F32)).astype(BF16)


def product(first, second):
    return jnp.dot(first, second, preferred_element_type=F32)


EXCHANGES = (4, 1, 1, 1, 1, 3, 6)
GATHERS = 3
OPERANDS = 11


def kernel(
    parts,
    *refs,
):
    operands, (state_ref, pressure_ref) = refs[:OPERANDS], refs[OPERANDS : OPERANDS + 2]
    held = refs[OPERANDS + 2 : 2 * OPERANDS + 2]
    load_sem, *scratch = refs[2 * OPERANDS + 2 :]
    loads = [
        pltpu.make_async_copy(source, here, load_sem.at[index])
        for index, (source, here) in enumerate(zip(operands, held))
    ]
    for load in loads:
        load.start()
    (
        flow_ref,
        left_exact_ref,
        right_exact_ref,
        plain_ref,
        roof_ref,
        old_ref,
        rows_ref,
        left_ref,
        right_ref,
        vertex_ref,
        modes_ref,
    ) = held

    parts_x, parts_y = parts
    devices = parts_x * parts_y
    count = len(EXCHANGES)
    fields = scratch[0:count]
    y_out = scratch[count : 2 * count]
    c_out = scratch[2 * count : 3 * count]
    x_in = scratch[3 * count : 4 * count]
    y_in = scratch[4 * count : 5 * count]
    c_in = scratch[5 * count : 6 * count]
    row_out, gathered, send_sem, recv_sem, row_send, row_recv = scratch[6 * count :]
    height = old_ref.shape[1]
    points = old_ref.shape[0]

    my_x, my_y = lax.axis_index("gx"), lax.axis_index("gy")
    me = my_x * parts_y + my_y

    barrier = pltpu.get_barrier_semaphore()

    def each_other(action):
        if devices <= 64:
            all_x = [lax.rem(my_x + step, parts_x) for step in range(parts_x)]
            all_y = [lax.rem(my_y + step, parts_y) for step in range(parts_y)]
            for step in range(1, devices):
                action(all_x[step // parts_y], all_y[step % parts_y])
            return

        def one(step, carry):
            other = lax.rem(me + step, devices)
            action(other // parts_y, lax.rem(other, parts_y))
            return carry

        lax.fori_loop(1, devices, one, 0)

    def greet(other_x, other_y):
        pl.semaphore_signal(barrier, inc=1, device_id=(other_x, other_y), device_id_type=MESH)

    each_other(greet)

    before_x, after_x = lax.rem(my_x + parts_x - 1, parts_x), lax.rem(my_x + 1, parts_x)
    before_y, after_y = lax.rem(my_y + parts_y - 1, parts_y), lax.rem(my_y + 1, parts_y)

    def block(which):
        return plain_ref[which * points : (which + 1) * points, :]

    def left_exact(values, first, last):
        high, low = split(values)
        stacked = jnp.concatenate([high, low, high, low, high], axis=0)
        return product(left_exact_ref[first * points : last * points, :], stacked)

    def right_exact(values, first, last):
        high, low = split(values)
        stacked = jnp.concatenate([high, low, high, low, high], axis=1)
        return product(stacked, right_exact_ref[:, first * height : last * height])

    def left(values, first, last):
        high, low = split(values)
        stacked = jnp.concatenate([high, low, high, low], axis=0)
        return product(left_ref[first * points : last * points, :], stacked)

    def right(values, first, last):
        high, low = split(values)
        stacked = jnp.concatenate([high, low, high], axis=1)
        return product(stacked, right_ref[:, first * height : last * height])

    lane = lax.broadcasted_iota(jnp.int32, (points, height), 1)
    joins_up = (lax.rem(lane, N) == N - 1) & (lane < height - 1)
    joins_down = (lax.rem(lane, N) == 0) & (lane > 0)

    def pair_z(values):
        up = pltpu.roll(values, height - 1, 1)
        down = pltpu.roll(values, 1, 1)
        return values + jnp.where(joins_up, up, jnp.where(joins_down, down, 0.0))

    def copies(which):
        field, number = fields[which], EXCHANGES[which]
        plan = []
        x_faces = (field.at[:, points - N : points, :], field.at[:, 0:N, :])
        for side, target in ((0, after_x), (1, before_x)):
            plan.append((x_faces[side], x_in[which].at[side], (target, my_y)))
        for side, target in ((0, after_y), (1, before_y)):
            plan.append((y_out[which].at[side], y_in[which].at[side], (my_x, target)))
        for corner, target in enumerate(
            ((after_x, after_y), (after_x, before_y), (before_x, after_y), (before_x, before_y))
        ):
            plan.append((c_out[which].at[corner], c_in[which].at[corner], target))
        return [
            pltpu.make_async_remote_copy(
                src_ref=source,
                dst_ref=landing,
                send_sem=send_sem.at[which, index],
                recv_sem=recv_sem.at[which, index],
                device_id=target,
                device_id_type=MESH,
            )
            for index, (source, landing, target) in enumerate(plan)
        ]

    def start(which, values):
        field, number = fields[which], EXCHANGES[which]
        values = [pair_z(value) for value in values]
        for index, value in enumerate(values):
            field[index] = value
            solid = value.reshape(N, N, height)
            y_out[which][0, index * N : index * N + N, :] = solid[:, N - 1, :]
            y_out[which][1, index * N : index * N + N, :] = solid[:, 0, :]
            for corner, row in enumerate((points - 1, points - N, N - 1, 0)):
                c_out[which][corner, index : index + 1, :] = value[row : row + 1, :]
        plan = copies(which)
        for copy in plan:
            copy.start()
        return values

    row_of_x = lax.broadcasted_iota(jnp.int32, (N, height), 0)

    def finish(which, values):
        plan = copies(which)
        for copy in plan:
            copy.wait_recv()
        results = []
        for index, value in enumerate(values):
            solid = value.reshape(N, N, height)
            from_x = x_in[which][:, index]
            first_y = y_in[which][0, index * N : index * N + N, :]
            last_y = y_in[which][1, index * N : index * N + N, :]
            corner = [c_in[which][which_one, index : index + 1, :] for which_one in range(4)]
            first_y = first_y + jnp.where(row_of_x == 0, corner[0], 0.0)
            last_y = last_y + jnp.where(row_of_x == 0, corner[1], 0.0)
            first_y = first_y + jnp.where(row_of_x == N - 1, corner[2], 0.0)
            last_y = last_y + jnp.where(row_of_x == N - 1, corner[3], 0.0)
            slabs = []
            for x in range(N):
                slab = solid[x]
                if x == 0:
                    slab = slab + from_x[0]
                if x == N - 1:
                    slab = slab + from_x[1]
                slab = slab + jnp.where(row_of_x == 0, first_y[x : x + 1, :], 0.0)
                slab = slab + jnp.where(row_of_x == N - 1, last_y[x : x + 1, :], 0.0)
                slabs.append(slab)
            results.append(jnp.concatenate(slabs, axis=0))
        return results

    def spread(which, row):
        row_out[which] = row
        gathered[which, pl.ds(me, 1), :] = row

        def send(other_x, other_y):
            pltpu.make_async_remote_copy(
                src_ref=row_out.at[which],
                dst_ref=gathered.at[which, pl.ds(me, 1), :],
                send_sem=row_send.at[which],
                recv_sem=row_recv.at[which],
                device_id=(other_x, other_y),
                device_id_type=MESH,
            ).start()

        each_other(send)

    def all_rows(which):
        return pltpu.make_async_remote_copy(
            src_ref=gathered.at[which, pl.ds(0, devices - 1), :],
            dst_ref=gathered.at[which, pl.ds(0, devices - 1), :],
            send_sem=row_send.at[which],
            recv_sem=row_recv.at[which],
            device_id=(after_x, my_y),
            device_id_type=MESH,
        )

    def collect(which):
        all_rows(which).wait_recv()
        return gathered[which]

    one_row = lax.broadcasted_iota(jnp.int32, (1, height), 1)
    group = height // 4
    spare = height // N + 1

    def operate(values):
        xy = left_exact(values, DX, KXY + 1)
        z = right_exact(values, ZD, ZK + 1)
        image = xy[2 * points :] * weight_z + weight_xy * z[:, height:]
        gradient = [mass * xy[:points], mass * xy[points : 2 * points], mass * z[:, :height]]
        return image + helmholtz_shift * mass * values, gradient

    def coarse_row(part):
        high, low, rest = split_thrice(part)
        stacked = jnp.concatenate([high, low, high, low, rest], axis=1)
        table = right_exact_ref[:, ZRESTRICT * height : (ZRESTRICT + 1) * height]
        terms = block(CORNERS) * product(stacked, table)
        return jnp.sum(terms, axis=0, keepdims=True)

    def with_scalars(row, residual, smoothed, image):
        gamma = jnp.sum(residual * smoothed * block(COPIES), axis=0, keepdims=True)
        delta = jnp.sum(smoothed * image, axis=0, keepdims=True)
        gamma = jnp.sum(gamma, axis=1, keepdims=True)
        delta = jnp.sum(delta, axis=1, keepdims=True)
        return jnp.where(one_row == spare, gamma, jnp.where(one_row == spare + 1, delta, row))

    def scalars(rows):
        total = jnp.sum(rows, axis=0, keepdims=True)
        return total[:, spare : spare + 1], total[:, spare + 1 : spare + 2]

    def local_solve(residual):
        modal = right(left(residual, FORWARD, FORWARD + 1), ZFORWARD, ZFORWARD + 1)
        modal = modal * block(SPECTRUM)
        return left(right(modal, ZBACK, ZBACK + 1), BACK, BACK + 1)

    def own_modes(piece):
        sides = block(SIDES)
        next_x, next_y = lax.rem(my_x + 1, parts_x), lax.rem(my_y + 1, parts_y)

        def row(which):
            return rows_ref[piece, pl.ds(which, 1), :]

        own_x = sides[:, 0:1] * row(my_x) + sides[:, 1:2] * row(next_x)
        own_y = sides[:, 2:3] * row(parts_x + my_y) + sides[:, 3:4] * row(parts_x + next_y)
        return split(own_x * own_y)

    pieces = modes_ref.shape[0]
    length = modes_ref.shape[1]
    span = length if pieces == 1 else 2 * length
    mode_lane = lax.broadcasted_iota(jnp.int32, (length, height), 1)

    def coarse_piece(piece, stacked, own):
        each = product(vertex_ref[piece, :, :span], stacked[:span])
        for begin in range(span, devices, span):
            lines = slice(begin, begin + span)
            each = each + product(vertex_ref[piece, :, lines], stacked[lines])
        tops, lows = each[: 4 * length], each[4 * length :]
        each = (tops[:, 2 * height :] + lows[:, height : 2 * height]) + (
            tops[:, height : 2 * height] + lows[:, :height]
        )
        each = each + tops[:, :height]
        total = jnp.zeros((length, height), F32)
        for corner in range(4):
            chosen = (mode_lane >= corner * group) & (mode_lane < corner * group + group)
            total = jnp.where(chosen, each[corner * length : (corner + 1) * length], total)
        levels = right(total * modes_ref[piece], ZPROLONG, ZPROLONG + 1)
        high, low = split(levels)
        own_high, own_low = own
        return product(own_high, high) + (product(own_high, low) + product(own_low, high))

    def coarse_solve(rows):
        stacked = jnp.concatenate(split_thrice(rows), axis=1)
        if pieces == 1:
            return coarse_piece(0, stacked, own)
        total = jnp.zeros((points, height), F32)
        for piece in range(pieces):
            total = total + coarse_piece(piece, stacked, own_modes(piece))
        return total

    for load in loads[:5]:
        load.wait()
    mass, weight_xy, weight_z = block(MASS), block(WXY), block(WZ)
    flow = [flow_ref[part * points : (part + 1) * points, :] for part in range(4)]
    u, v, w, theta = flow
    xy = left_exact(jnp.concatenate(flow, axis=1), DX, KXY + 1)
    z = right_exact(flow_ref[...], ZD, ZK + 1)
    canopy = jnp.where(lane // N < roof_ref[...], 1.0, 0.0)
    drag = drag_strength * canopy * jnp.sqrt(u * u + v * v + w * w)
    forcing = [-drag * u, -drag * v, -drag * w + buoyancy * theta, heating * canopy]
    rates = []
    for part in range(4):
        lanes = slice(part * height, (part + 1) * height)
        rows = slice(part * points, (part + 1) * points)
        advection = u * xy[:points, lanes] + v * xy[points : 2 * points, lanes] + w * z[rows, :height]
        friction = xy[2 * points :, lanes] * weight_z + weight_xy * z[rows, height:]
        rates.append(mass * (forcing[part] - advection) - viscosity * friction)
    pl.semaphore_wait(barrier, devices - 1)
    rates = start(0, rates)

    for load in loads[5:]:
        load.wait()
    old = old_ref[...]
    old_image, old_gradient = operate(old)
    own = own_modes(0) if pieces == 1 else None

    rates = finish(0, rates)
    step = block(STEP)
    provisional = [values + step * rate for values, rate in zip(flow, rates)]
    provisional[2] = jnp.where((lane == 0) | (lane == height - 1), 0.0, provisional[2])
    divergence = (
        left_exact(provisional[0], DX, DX + 1)
        + left_exact(provisional[1], DY, DY + 1)
        + right_exact(provisional[2], ZD, ZD + 1)
    )
    raw = -mass * divergence - old_image
    whole = start(1, [raw])
    spread(0, coarse_row(raw))
    residual = finish(1, whole)[0]

    local = start(2, [local_solve(residual)])
    coarse = coarse_solve(collect(0))
    first = finish(2, local)[0] + coarse
    raw, first_gradient = operate(first)
    image = start(3, [raw])
    spread(1, with_scalars(coarse_row(raw), residual, first, raw))
    gradients = start(6, old_gradient + first_gradient)
    image = finish(3, image)[0]

    local = start(4, [local_solve(image)])
    rows = collect(1)
    coarse = coarse_solve(rows)
    gamma_first, delta_first = scalars(rows)
    alpha_first = gamma_first / delta_first
    residual = residual - alpha_first * image
    second = first - alpha_first * (finish(4, local)[0] + coarse)
    raw, second_gradient = operate(second)
    spread(2, with_scalars(jnp.zeros((1, height), F32), residual, second, raw))
    second_gradient = start(5, second_gradient)
    gradients = finish(6, gradients)
    gamma, delta = scalars(collect(2))
    ratio = gamma / gamma_first
    alpha = gamma / (delta - ratio * gamma / alpha_first)
    weight_first = alpha_first + alpha * ratio
    pressure_ref[...] = old + weight_first * first + alpha * second
    state_ref[3 * points : 4 * points, :] = provisional[3]
    second_gradient = finish(5, second_gradient)
    inverse = block(INVERSE)
    for part in range(3):
        total = gradients[part] + weight_first * gradients[3 + part] + alpha * second_gradient[part]
        state_ref[part * points : (part + 1) * points, :] = provisional[part] - total * inverse

    for which in range(count):
        for copy in copies(which):
            copy.wait_send()
    for which in range(GATHERS):
        all_rows(which).wait_send()


def on_device(flow_state, building_height, pressure_old):
    parts = (lax.axis_size("gx"), lax.axis_size("gy"))
    devices = parts[0] * parts[1]
    components, width, depth, height = flow_state.shape
    points = width * depth
    assert width == N and depth == N and components == 4
    tables = constants(parts[0], parts[1], height)
    left_exact, right_exact, left, right, plain, vertex, rows, modes = [
        jnp.asarray(table) for table in tables
    ]
    operands = [
        flow_state.reshape(components * points, height),
        left_exact,
        right_exact,
        plain,
        building_height,
        pressure_old.reshape(points, height),
        rows,
        left,
        right,
        vertex,
        modes,
    ]
    scratch = [pltpu.VMEM(operand.shape, operand.dtype) for operand in operands]
    scratch += [pltpu.SemaphoreType.DMA((len(operands),))]
    scratch += [pltpu.VMEM((number, points, height), F32) for number in EXCHANGES]
    scratch += [pltpu.VMEM((2, number * N, height), F32) for number in EXCHANGES]
    scratch += [pltpu.VMEM((4, number, height), F32) for number in EXCHANGES]
    scratch += [pltpu.VMEM((2, number, N, height), F32) for number in EXCHANGES]
    scratch += [pltpu.VMEM((2, number * N, height), F32) for number in EXCHANGES]
    scratch += [pltpu.VMEM((4, number, height), F32) for number in EXCHANGES]
    scratch += [
        pltpu.VMEM((GATHERS, 1, height), F32),
        pltpu.VMEM((GATHERS, devices, height), F32),
        pltpu.SemaphoreType.DMA((len(EXCHANGES), 8)),
        pltpu.SemaphoreType.DMA((len(EXCHANGES), 8)),
        pltpu.SemaphoreType.DMA((GATHERS,)),
        pltpu.SemaphoreType.DMA((GATHERS,)),
    ]
    whole = pl.BlockSpec(memory_space=pltpu.VMEM)
    state, pressure = pl.pallas_call(
        functools.partial(kernel, parts),
        out_shape=(
            jax.ShapeDtypeStruct((components * points, height), F32),
            jax.ShapeDtypeStruct((points, height), F32),
        ),
        in_specs=[pl.BlockSpec(memory_space=pltpu.HBM)] * len(operands),
        out_specs=(whole, whole),
        scratch_shapes=scratch,
        compiler_params=pltpu.CompilerParams(
            collective_id=0, has_side_effects=True, vmem_limit_bytes=48 * 2**20
        ),
    )(*operands)
    return state.reshape(flow_state.shape), pressure.reshape(pressure_old.shape)


def solution(mesh):
    in_specs = (P(None, "gx", "gy", None), P("gx", "gy"), P("gx", "gy", None))
    out_specs = (P(None, "gx", "gy", None), P("gx", "gy", None))
    return jax.shard_map(
        on_device, mesh=mesh, in_specs=in_specs, out_specs=out_specs, check_vma=False
    )
```

```python
import functools
import math

import jax
import jax.numpy as jnp
import ml_dtypes
import numpy as np
from jax import lax
from jax.experimental import pallas as pl
from jax.experimental.pallas import tpu as pltpu
from jax.sharding import PartitionSpec as P

F32 = jnp.float32
BF16 = jnp.bfloat16
MESH = pl.DeviceIdType.MESH
N = 8
viscosity = 0.05
time_step = 0.01
drag_strength = 20.0
heating = 40.0
buoyancy = 10.0
helmholtz_shift = 0.001
local_shift = 0.5
coarse_shift = 0.02
gll_points = (
    -1.0,
    -0.8717401485096066,
    -0.5917001814331423,
    -0.2092992179024789,
    0.2092992179024789,
    0.5917001814331423,
    0.8717401485096066,
    1.0,
)


def legendre_seven(points):
    squared = points * points
    return points * (((429.0 * squared - 693.0) * squared + 315.0) * squared - 35.0) / 16.0


def jacobi_eigen(matrix):
    current = np.array(matrix)
    basis = np.eye(8)
    for rounds in range(12):
        for first in range(7):
            for second in range(first + 1, 8):
                rotation_angle = 0.5 * math.atan2(
                    2.0 * float(current[first, second]),
                    float(current[second, second] - current[first, first]),
                )
                cosine = math.cos(rotation_angle)
                sine = math.sin(rotation_angle)
                rotation = np.eye(8)
                rotation[first, first] = cosine
                rotation[second, second] = cosine
                rotation[first, second] = sine
                rotation[second, first] = -sine
                current = rotation.T @ current @ rotation
                basis = basis @ rotation
    return (np.sum(current * np.eye(8), axis=0), basis)


def gll_tables():
    gll_nodes = np.array(gll_points)
    values = legendre_seven(gll_nodes)
    weights = 2.0 / (56.0 * values * values)
    differ = gll_nodes[:, None] - gll_nodes[None, :] + np.eye(8)
    derivative = values[:, None] / values[None, :] / differ * (1.0 - np.eye(8))
    derivative = (
        derivative + np.eye(8) * np.array([-14.0, 0.0, 0.0, 0.0, 0.0, 0.0, 0.0, 14.0])[None, :]
    )
    stiffness = derivative.T @ (weights[:, None] * derivative)
    scaled = stiffness / np.sqrt(np.outer(weights, weights))
    scaled = 0.5 * (scaled + scaled.T)
    eigen_values, eigen_vectors = jacobi_eigen(scaled)
    eigen_basis = eigen_vectors / np.sqrt(weights)[:, None]
    return (gll_nodes, weights, derivative, eigen_basis, np.maximum(eigen_values, 0.0))


def hartley_tables(count):
    index = np.arange(count)
    angle = 2.0 * np.pi / count * (index[:, None] * index[None, :] % count)
    hartley = (np.cos(angle) + np.sin(angle)) / np.sqrt(count)
    return hartley, 2.0 - 2.0 * np.cos(2.0 * np.pi / count * index)


def cosine_tables(count):
    index = np.arange(count)
    angle = np.pi / count * (index[:, None] + 0.5) * index[None, :]
    norms = np.where(index == 0, np.sqrt(1.0 / count), np.sqrt(2.0 / count))
    return np.cos(angle) * norms[None, :], 2.0 - 2.0 * np.cos(np.pi / count * index)


def thirds(matrix):
    pieces = []
    for piece in range(3):
        pieces.append(matrix.astype(np.float32).astype(ml_dtypes.bfloat16))
        matrix = matrix - pieces[-1].astype(np.float64)
    return pieces


def mode_pieces(modes):
    return modes // 128 if modes > 128 and modes % 128 == 0 else 1


DX, DY, KXY = range(3)
ZD, ZK, ZRESTRICT = range(3)
FORWARD, BACK = range(2)
ZFORWARD, ZBACK, ZPROLONG = range(3)
MASS, WXY, WZ, STEP, INVERSE, COPIES, SPECTRUM, CORNERS, SIDES = range(9)


@functools.lru_cache(maxsize=None)
def constants(parts_x, parts_y, height):
    nodes, weights, derivative, basis, values = gll_tables()
    layers = height // N
    levels = layers + 1
    group = height // 4
    assert levels + 2 <= group
    eye = np.eye(N)
    diagonal = np.diag(weights)
    stiffness = derivative.T @ diagonal @ derivative

    lefts = np.concatenate(
        [
            np.kron(derivative, eye),
            np.kron(eye, derivative),
            np.kron(stiffness, diagonal) + np.kron(diagonal, stiffness),
        ],
        axis=0,
    )
    high, low, rest = thirds(lefts)
    left_exact = np.concatenate([high, high, low, low, rest], axis=1)
    high, low, rest = thirds(np.concatenate([np.kron(basis.T, basis.T), np.kron(basis, basis)]))
    left_table = np.concatenate([high, high, low, low], axis=1)

    near, far = (1.0 - nodes) / 2.0, (1.0 + nodes) / 2.0
    vertical = np.zeros((height, levels))
    for layer in range(layers):
        vertical[layer * N : layer * N + N, layer] = near
        vertical[layer * N : layer * N + N, layer + 1] = far
    cosine, eigen_z = cosine_tables(levels)
    prolong_z = vertical @ cosine
    place = np.arange(height)
    face = np.where((np.arange(N) == 0) | (np.arange(N) == N - 1), 2.0, 1.0)
    count_z = np.where((place == 0) | (place == height - 1), 1.0, np.tile(face, layers))
    grouped = np.zeros((height, 4, group))
    grouped[:, :, :levels] = prolong_z[:, None, :]
    grouped = grouped.reshape(height, height)
    many = np.eye(layers)
    rights = [np.kron(many, derivative.T), np.kron(many, stiffness)]
    high, low, rest = thirds(np.concatenate(rights, axis=1))
    right_exact = np.concatenate([high, high, low, low, rest], axis=0)
    high, low, rest = thirds(grouped)
    right_exact = np.concatenate(
        [right_exact, np.concatenate([high, high, low, low, high], axis=0)], axis=1
    )
    rights = [np.kron(many, basis), np.kron(many, basis.T), grouped.T]
    high, low, rest = thirds(np.concatenate(rights, axis=1))
    right_table = np.concatenate([high, high, low], axis=0)

    weight_xy = np.kron(weights, weights)[:, None] * np.ones((1, height))
    weight_z = np.ones((N * N, 1)) * np.tile(weights, layers)[None, :]
    mass = weight_xy * weight_z
    count_xy = np.kron(face, face)
    copies = count_xy[:, None] * count_z[None, :]
    spectrum = (values[:, None] + values[None, :]).reshape(-1)[:, None] + np.tile(values, layers)
    near_x, far_x = np.repeat(near, N), np.repeat(far, N)
    near_y, far_y = np.tile(near, N), np.tile(far, N)
    sides = np.zeros((N * N, height))
    sides[:, 0], sides[:, 1], sides[:, 2], sides[:, 3] = near_x, far_x, near_y, far_y
    corner = np.stack([near_x * near_y, near_x * far_y, far_x * near_y, far_x * far_y], axis=1)
    corners = np.repeat(corner, group, axis=1)
    plain = np.concatenate(
        [
            mass,
            weight_xy,
            weight_z,
            time_step / (mass * copies),
            1.0 / (mass * copies),
            1.0 / copies,
            1.0 / (spectrum + local_shift),
            corners,
            sides,
        ],
        axis=0,
    ).astype(np.float32)

    hartley_x, eigen_x = hartley_tables(parts_x)
    hartley_y, eigen_y = hartley_tables(parts_y)
    vertex = []
    for step_x in (0, 1):
        for step_y in (0, 1):
            vertex.append(
                np.kron(np.roll(hartley_x, -step_x, axis=1), np.roll(hartley_y, -step_y, axis=1))
            )
    modes = parts_x * parts_y
    pieces = mode_pieces(modes)
    high, low, rest = thirds(np.stack(vertex))
    vertex_table = np.stack([high, low]).reshape(8, pieces, modes // pieces, modes)
    vertex_table = vertex_table.transpose(1, 0, 2, 3).reshape(pieces, -1, modes)
    rows = np.concatenate(
        [np.repeat(hartley_x, parts_y, axis=1), np.tile(hartley_y, (1, parts_x))], axis=0
    ).astype(np.float32)
    rows = rows.reshape(parts_x + parts_y, pieces, -1).transpose(1, 0, 2)
    horizontal = (eigen_x[:, None] + eigen_y[None, :]).reshape(-1)
    inverse = np.zeros((modes, 4, group))
    inverse[:, :, :levels] = (
        1.0 / (2.0 * (horizontal[:, None] + eigen_z[None, :]) + coarse_shift)
    )[:, None, :]
    inverse = inverse.reshape(pieces, -1, height).astype(np.float32)
    return left_exact, right_exact, left_table, right_table, plain, vertex_table, rows, inverse


def split(values):
    high = values.astype(BF16)
    return high, (values - high.astype(F32)).astype(BF16)


def split_thrice(values):
    high = values.astype(BF16)
    rest = values - high.astype(F32)
    low = rest.astype(BF16)
    return high, low, (rest - low.astype(F32)).astype(BF16)


def product(first, second):
    return jnp.dot(first, second, preferred_element_type=F32)


EXCHANGES = (4, 4, 1, 1, 4, 3)
GATHERS = 3
OPERANDS = 11


def kernel(
    parts,
    *refs,
):
    operands, (state_ref, pressure_ref) = refs[:OPERANDS], refs[OPERANDS : OPERANDS + 2]
    held = refs[OPERANDS + 2 : 2 * OPERANDS + 2]
    load_sem, *scratch = refs[2 * OPERANDS + 2 :]
    loads = [
        pltpu.make_async_copy(source, here, load_sem.at[index])
        for index, (source, here) in enumerate(zip(operands, held))
    ]
    for load in loads:
        load.start()
    (
        flow_ref,
        left_exact_ref,
        right_exact_ref,
        plain_ref,
        roof_ref,
        old_ref,
        rows_ref,
        left_ref,
        right_ref,
        vertex_ref,
        modes_ref,
    ) = held

    parts_x, parts_y = parts
    devices = parts_x * parts_y
    count = len(EXCHANGES)
    fields = scratch[0:count]
    y_out = scratch[count : 2 * count]
    c_out = scratch[2 * count : 3 * count]
    x_in = scratch[3 * count : 4 * count]
    y_in = scratch[4 * count : 5 * count]
    c_in = scratch[5 * count : 6 * count]
    row_out, gathered, send_sem, recv_sem, row_send, row_recv = scratch[6 * count :]
    height = old_ref.shape[1]
    points = old_ref.shape[0]

    my_x, my_y = lax.axis_index("gx"), lax.axis_index("gy")
    me = my_x * parts_y + my_y

    barrier = pltpu.get_barrier_semaphore()

    def each_other(action):
        if devices <= 64:
            all_x = [lax.rem(my_x + step, parts_x) for step in range(parts_x)]
            all_y = [lax.rem(my_y + step, parts_y) for step in range(parts_y)]
            for step in range(1, devices):
                action(all_x[step // parts_y], all_y[step % parts_y])
            return

        def one(step, carry):
            other = lax.rem(me + step, devices)
            action(other // parts_y, lax.rem(other, parts_y))
            return carry

        lax.fori_loop(1, devices, one, 0)

    def greet(other_x, other_y):
        pl.semaphore_signal(barrier, inc=1, device_id=(other_x, other_y), device_id_type=MESH)

    each_other(greet)

    before_x, after_x = lax.rem(my_x + parts_x - 1, parts_x), lax.rem(my_x + 1, parts_x)
    before_y, after_y = lax.rem(my_y + parts_y - 1, parts_y), lax.rem(my_y + 1, parts_y)

    def block(which):
        return plain_ref[which * points : (which + 1) * points, :]

    def left_exact(values, first, last):
        high, low = split(values)
        stacked = jnp.concatenate([high, low, high, low, high], axis=0)
        return product(left_exact_ref[first * points : last * points, :], stacked)

    def right_exact(values, first, last):
        high, low = split(values)
        stacked = jnp.concatenate([high, low, high, low, high], axis=1)
        return product(stacked, right_exact_ref[:, first * height : last * height])

    def left(values, first, last):
        high, low = split(values)
        stacked = jnp.concatenate([high, low, high, low], axis=0)
        return product(left_ref[first * points : last * points, :], stacked)

    def right(values, first, last):
        high, low = split(values)
        stacked = jnp.concatenate([high, low, high], axis=1)
        return product(stacked, right_ref[:, first * height : last * height])

    lane = lax.broadcasted_iota(jnp.int32, (points, height), 1)
    joins_up = (lax.rem(lane, N) == N - 1) & (lane < height - 1)
    joins_down = (lax.rem(lane, N) == 0) & (lane > 0)

    def pair_z(values):
        up = pltpu.roll(values, height - 1, 1)
        down = pltpu.roll(values, 1, 1)
        return values + jnp.where(joins_up, up, jnp.where(joins_down, down, 0.0))

    def copies(which):
        field = fields[which]
        plan = []
        x_faces = (field.at[:, points - N : points, :], field.at[:, 0:N, :])
        for side, target in ((0, after_x), (1, before_x)):
            plan.append((x_faces[side], x_in[which].at[side], (target, my_y)))
        for corner, target in enumerate(
            ((after_x, after_y), (after_x, before_y), (before_x, after_y), (before_x, before_y))
        ):
            plan.append((c_out[which].at[corner], c_in[which].at[corner], target))
        for side, target in ((0, after_y), (1, before_y)):
            plan.append((y_out[which].at[side], y_in[which].at[side], (my_x, target)))
        return [
            pltpu.make_async_remote_copy(
                src_ref=source,
                dst_ref=landing,
                send_sem=send_sem.at[which, index],
                recv_sem=recv_sem.at[which, index],
                device_id=target,
                device_id_type=MESH,
            )
            for index, (source, landing, target) in enumerate(plan)
        ]

    def stage(which, values, first=0):
        values = [pair_z(value) for value in values]
        for index, value in enumerate(values, first):
            fields[which][index] = value
            solid = value.reshape(N, N, height)
            y_out[which][0, index * N : index * N + N, :] = solid[:, N - 1, :]
            y_out[which][1, index * N : index * N + N, :] = solid[:, 0, :]
            for corner, row in enumerate((points - 1, points - N, N - 1, 0)):
                c_out[which][corner, index : index + 1, :] = value[row : row + 1, :]
        return values

    def start(which, values):
        values = stage(which, values)
        for copy in copies(which):
            copy.start()
        return values

    row_of_x = lax.broadcasted_iota(jnp.int32, (N, height), 0)

    def finish(which, values):
        for copy in copies(which):
            copy.wait_recv()
        return join(which, values)

    def join(which, values, first=0):
        results = []
        for index, value in enumerate(values, first):
            solid = value.reshape(N, N, height)
            from_x = x_in[which][:, index]
            first_y = y_in[which][0, index * N : index * N + N, :]
            last_y = y_in[which][1, index * N : index * N + N, :]
            corner = [c_in[which][which_one, index : index + 1, :] for which_one in range(4)]
            first_y = first_y + jnp.where(row_of_x == 0, corner[0], 0.0)
            last_y = last_y + jnp.where(row_of_x == 0, corner[1], 0.0)
            first_y = first_y + jnp.where(row_of_x == N - 1, corner[2], 0.0)
            last_y = last_y + jnp.where(row_of_x == N - 1, corner[3], 0.0)
            slabs = []
            for x in range(N):
                slab = solid[x]
                if x == 0:
                    slab = slab + from_x[0]
                if x == N - 1:
                    slab = slab + from_x[1]
                slab = slab + jnp.where(row_of_x == 0, first_y[x : x + 1, :], 0.0)
                slab = slab + jnp.where(row_of_x == N - 1, last_y[x : x + 1, :], 0.0)
                slabs.append(slab)
            results.append(jnp.concatenate(slabs, axis=0))
        return results

    def spread(which, row):
        row_out[which] = row
        gathered[which, pl.ds(me, 1), :] = row

        def send(other_x, other_y):
            pltpu.make_async_remote_copy(
                src_ref=row_out.at[which],
                dst_ref=gathered.at[which, pl.ds(me, 1), :],
                send_sem=row_send.at[which],
                recv_sem=row_recv.at[which],
                device_id=(other_x, other_y),
                device_id_type=MESH,
            ).start()

        each_other(send)

    def all_rows(which):
        return pltpu.make_async_remote_copy(
            src_ref=gathered.at[which, pl.ds(0, devices - 1), :],
            dst_ref=gathered.at[which, pl.ds(0, devices - 1), :],
            send_sem=row_send.at[which],
            recv_sem=row_recv.at[which],
            device_id=(after_x, my_y),
            device_id_type=MESH,
        )

    def collect(which):
        all_rows(which).wait_recv()
        return gathered[which]

    one_row = lax.broadcasted_iota(jnp.int32, (1, height), 1)
    group = height // 4
    spare = height // N + 1

    def operate(values):
        xy = left_exact(values, DX, KXY + 1)
        z = right_exact(values, ZD, ZK + 1)
        image = xy[2 * points :] * weight_z + weight_xy * z[:, height:]
        gradient = [mass * xy[:points], mass * xy[points : 2 * points], mass * z[:, :height]]
        return image + helmholtz_shift * mass * values, gradient

    def coarse_row(part):
        high, low, rest = split_thrice(part)
        stacked = jnp.concatenate([high, low, high, low, rest], axis=1)
        table = right_exact_ref[:, ZRESTRICT * height : (ZRESTRICT + 1) * height]
        terms = block(CORNERS) * product(stacked, table)
        return jnp.sum(terms, axis=0, keepdims=True)

    def with_scalars(row, residual, smoothed, image):
        gamma = jnp.sum(residual * smoothed * block(COPIES), axis=0, keepdims=True)
        delta = jnp.sum(smoothed * image, axis=0, keepdims=True)
        gamma = jnp.sum(gamma, axis=1, keepdims=True)
        delta = jnp.sum(delta, axis=1, keepdims=True)
        return jnp.where(one_row == spare, gamma, jnp.where(one_row == spare + 1, delta, row))

    def scalars(rows):
        total = jnp.sum(rows, axis=0, keepdims=True)
        return total[:, spare : spare + 1], total[:, spare + 1 : spare + 2]

    def local_solve(residual):
        modal = right(left(residual, FORWARD, FORWARD + 1), ZFORWARD, ZFORWARD + 1)
        modal = modal * block(SPECTRUM)
        return left(right(modal, ZBACK, ZBACK + 1), BACK, BACK + 1)

    def own_modes(piece):
        sides = block(SIDES)
        next_x, next_y = lax.rem(my_x + 1, parts_x), lax.rem(my_y + 1, parts_y)

        def row(which):
            return rows_ref[piece, pl.ds(which, 1), :]

        own_x = sides[:, 0:1] * row(my_x) + sides[:, 1:2] * row(next_x)
        own_y = sides[:, 2:3] * row(parts_x + my_y) + sides[:, 3:4] * row(parts_x + next_y)
        return split(own_x * own_y)

    pieces = modes_ref.shape[0]
    length = modes_ref.shape[1]
    span = length if pieces == 1 else 2 * length
    mode_lane = lax.broadcasted_iota(jnp.int32, (length, height), 1)

    def coarse_piece(piece, stacked, own):
        each = product(vertex_ref[piece, :, :span], stacked[:span])
        for begin in range(span, devices, span):
            lines = slice(begin, begin + span)
            each = each + product(vertex_ref[piece, :, lines], stacked[lines])
        tops, lows = each[: 4 * length], each[4 * length :]
        each = (tops[:, 2 * height :] + lows[:, height : 2 * height]) + (
            tops[:, height : 2 * height] + lows[:, :height]
        )
        each = each + tops[:, :height]
        total = jnp.zeros((length, height), F32)
        for corner in range(4):
            chosen = (mode_lane >= corner * group) & (mode_lane < corner * group + group)
            total = jnp.where(chosen, each[corner * length : (corner + 1) * length], total)
        levels = right(total * modes_ref[piece], ZPROLONG, ZPROLONG + 1)
        high, low = split(levels)
        own_high, own_low = own
        return product(own_high, high) + (product(own_high, low) + product(own_low, high))

    def coarse_solve(rows):
        stacked = jnp.concatenate(split_thrice(rows), axis=1)
        if pieces == 1:
            return coarse_piece(0, stacked, own)
        total = jnp.zeros((points, height), F32)
        for piece in range(pieces):
            total = total + coarse_piece(piece, stacked, own_modes(piece))
        return total

    for load in loads[:5]:
        load.wait()
    mass, weight_xy, weight_z = block(MASS), block(WXY), block(WZ)
    flow = [flow_ref[part * points : (part + 1) * points, :] for part in range(4)]
    u, v, w, theta = flow
    xy = left_exact(jnp.concatenate(flow, axis=1), DX, KXY + 1)
    z = right_exact(flow_ref[...], ZD, ZK + 1)
    canopy = jnp.where(lane // N < roof_ref[...], 1.0, 0.0)
    drag = drag_strength * canopy * jnp.sqrt(u * u + v * v + w * w)
    forcing = [-drag * u, -drag * v, -drag * w + buoyancy * theta, heating * canopy]
    rates = []
    for part in range(4):
        lanes = slice(part * height, (part + 1) * height)
        rows = slice(part * points, (part + 1) * points)
        advection = u * xy[:points, lanes] + v * xy[points : 2 * points, lanes] + w * z[rows, :height]
        friction = xy[2 * points :, lanes] * weight_z + weight_xy * z[rows, height:]
        rates.append(mass * (forcing[part] - advection) - viscosity * friction)
    pl.semaphore_wait(barrier, devices - 1)
    rates = start(0, rates)

    for load in loads[5:]:
        load.wait()
    old = old_ref[...]
    old_image, old_gradient = operate(old)
    old_gradient = stage(1, old_gradient, 1)
    own = own_modes(0) if pieces == 1 else None

    rates = finish(0, rates)
    step = block(STEP)
    provisional = [values + step * rate for values, rate in zip(flow, rates)]
    provisional[2] = jnp.where((lane == 0) | (lane == height - 1), 0.0, provisional[2])
    divergence = (
        left_exact(provisional[0], DX, DX + 1)
        + left_exact(provisional[1], DY, DY + 1)
        + right_exact(provisional[2], ZD, ZD + 1)
    )
    raw = -mass * divergence - old_image
    whole = start(1, [raw])
    spread(0, coarse_row(raw))
    residual = finish(1, whole)[0]

    local = start(2, [local_solve(residual)])
    coarse = coarse_solve(collect(0))
    first = finish(2, local)[0] + coarse
    raw, first_gradient = operate(first)
    image = start(3, [raw])
    spread(1, with_scalars(coarse_row(raw), residual, first, raw))
    first_gradient = stage(4, first_gradient, 1)
    image = finish(3, image)[0]

    local = start(4, [local_solve(image)])
    rows = collect(1)
    coarse = coarse_solve(rows)
    gamma_first, delta_first = scalars(rows)
    alpha_first = gamma_first / delta_first
    residual = residual - alpha_first * image
    second = first - alpha_first * (finish(4, local)[0] + coarse)
    raw, second_gradient = operate(second)
    spread(2, with_scalars(jnp.zeros((1, height), F32), residual, second, raw))
    second_gradient = start(5, second_gradient)
    gradients = join(1, old_gradient, 1) + join(4, first_gradient, 1)
    gamma, delta = scalars(collect(2))
    ratio = gamma / gamma_first
    alpha = gamma / (delta - ratio * gamma / alpha_first)
    weight_first = alpha_first + alpha * ratio
    pressure_ref[...] = old + weight_first * first + alpha * second
    state_ref[3 * points : 4 * points, :] = provisional[3]
    second_gradient = finish(5, second_gradient)
    inverse = block(INVERSE)
    for part in range(3):
        total = gradients[part] + weight_first * gradients[3 + part] + alpha * second_gradient[part]
        state_ref[part * points : (part + 1) * points, :] = provisional[part] - total * inverse

    for which in range(count):
        for copy in copies(which):
            copy.wait_send()
    for which in range(GATHERS):
        all_rows(which).wait_send()


def on_device(flow_state, building_height, pressure_old):
    parts = (lax.axis_size("gx"), lax.axis_size("gy"))
    devices = parts[0] * parts[1]
    components, width, depth, height = flow_state.shape
    points = width * depth
    assert width == N and depth == N and components == 4
    tables = constants(parts[0], parts[1], height)
    left_exact, right_exact, left, right, plain, vertex, rows, modes = [
        jnp.asarray(table) for table in tables
    ]
    operands = [
        flow_state.reshape(components * points, height),
        left_exact,
        right_exact,
        plain,
        building_height,
        pressure_old.reshape(points, height),
        rows,
        left,
        right,
        vertex,
        modes,
    ]
    scratch = [pltpu.VMEM(operand.shape, operand.dtype) for operand in operands]
    scratch += [pltpu.SemaphoreType.DMA((len(operands),))]
    scratch += [pltpu.VMEM((number, points, height), F32) for number in EXCHANGES]
    scratch += [pltpu.VMEM((2, number * N, height), F32) for number in EXCHANGES]
    scratch += [pltpu.VMEM((4, number, height), F32) for number in EXCHANGES]
    scratch += [pltpu.VMEM((2, number, N, height), F32) for number in EXCHANGES]
    scratch += [pltpu.VMEM((2, number * N, height), F32) for number in EXCHANGES]
    scratch += [pltpu.VMEM((4, number, height), F32) for number in EXCHANGES]
    scratch += [
        pltpu.VMEM((GATHERS, 1, height), F32),
        pltpu.VMEM((GATHERS, devices, height), F32),
        pltpu.SemaphoreType.DMA((len(EXCHANGES), 8)),
        pltpu.SemaphoreType.DMA((len(EXCHANGES), 8)),
        pltpu.SemaphoreType.DMA((GATHERS,)),
        pltpu.SemaphoreType.DMA((GATHERS,)),
    ]
    whole = pl.BlockSpec(memory_space=pltpu.VMEM)
    state, pressure = pl.pallas_call(
        functools.partial(kernel, parts),
        out_shape=(
            jax.ShapeDtypeStruct((components * points, height), F32),
            jax.ShapeDtypeStruct((points, height), F32),
        ),
        in_specs=[pl.BlockSpec(memory_space=pltpu.HBM)] * len(operands),
        out_specs=(whole, whole),
        scratch_shapes=scratch,
        compiler_params=pltpu.CompilerParams(
            collective_id=0, has_side_effects=True, vmem_limit_bytes=60 * 2**20
        ),
    )(*operands)
    return state.reshape(flow_state.shape), pressure.reshape(pressure_old.shape)


def solution(mesh):
    in_specs = (P(None, "gx", "gy", None), P("gx", "gy"), P("gx", "gy", None))
    out_specs = (P(None, "gx", "gy", None), P("gx", "gy", None))
    return jax.shard_map(
        on_device, mesh=mesh, in_specs=in_specs, out_specs=out_specs, check_vma=False
    )
```

```python
import functools
import math

import jax
import jax.numpy as jnp
import ml_dtypes
import numpy as np
from jax import lax
from jax.experimental import pallas as pl
from jax.experimental.pallas import tpu as pltpu
from jax.sharding import PartitionSpec as P

F32 = jnp.float32
BF16 = jnp.bfloat16
MESH = pl.DeviceIdType.MESH
N = 8
viscosity = 0.05
time_step = 0.01
drag_strength = 20.0
heating = 40.0
buoyancy = 10.0
helmholtz_shift = 0.001
local_shift = 0.5
coarse_shift = 0.02
gll_points = (
    -1.0,
    -0.8717401485096066,
    -0.5917001814331423,
    -0.2092992179024789,
    0.2092992179024789,
    0.5917001814331423,
    0.8717401485096066,
    1.0,
)


def legendre_seven(points):
    squared = points * points
    return points * (((429.0 * squared - 693.0) * squared + 315.0) * squared - 35.0) / 16.0


def jacobi_eigen(matrix):
    current = np.array(matrix)
    basis = np.eye(8)
    for rounds in range(12):
        for first in range(7):
            for second in range(first + 1, 8):
                rotation_angle = 0.5 * math.atan2(
                    2.0 * float(current[first, second]),
                    float(current[second, second] - current[first, first]),
                )
                cosine = math.cos(rotation_angle)
                sine = math.sin(rotation_angle)
                rotation = np.eye(8)
                rotation[first, first] = cosine
                rotation[second, second] = cosine
                rotation[first, second] = sine
                rotation[second, first] = -sine
                current = rotation.T @ current @ rotation
                basis = basis @ rotation
    return (np.sum(current * np.eye(8), axis=0), basis)


def gll_tables():
    gll_nodes = np.array(gll_points)
    values = legendre_seven(gll_nodes)
    weights = 2.0 / (56.0 * values * values)
    differ = gll_nodes[:, None] - gll_nodes[None, :] + np.eye(8)
    derivative = values[:, None] / values[None, :] / differ * (1.0 - np.eye(8))
    derivative = (
        derivative + np.eye(8) * np.array([-14.0, 0.0, 0.0, 0.0, 0.0, 0.0, 0.0, 14.0])[None, :]
    )
    stiffness = derivative.T @ (weights[:, None] * derivative)
    scaled = stiffness / np.sqrt(np.outer(weights, weights))
    scaled = 0.5 * (scaled + scaled.T)
    eigen_values, eigen_vectors = jacobi_eigen(scaled)
    eigen_basis = eigen_vectors / np.sqrt(weights)[:, None]
    return (gll_nodes, weights, derivative, eigen_basis, np.maximum(eigen_values, 0.0))


def hartley_tables(count):
    index = np.arange(count)
    angle = 2.0 * np.pi / count * (index[:, None] * index[None, :] % count)
    hartley = (np.cos(angle) + np.sin(angle)) / np.sqrt(count)
    return hartley, 2.0 - 2.0 * np.cos(2.0 * np.pi / count * index)


def cosine_tables(count):
    index = np.arange(count)
    angle = np.pi / count * (index[:, None] + 0.5) * index[None, :]
    norms = np.where(index == 0, np.sqrt(1.0 / count), np.sqrt(2.0 / count))
    return np.cos(angle) * norms[None, :], 2.0 - 2.0 * np.cos(np.pi / count * index)


def thirds(matrix):
    pieces = []
    for piece in range(3):
        pieces.append(matrix.astype(np.float32).astype(ml_dtypes.bfloat16))
        matrix = matrix - pieces[-1].astype(np.float64)
    return pieces


def mode_pieces(modes):
    return modes // 128 if modes > 128 and modes % 128 == 0 else 1


DX, DY, KXY = range(3)
ZD, ZK, ZRESTRICT = range(3)
FORWARD, BACK = range(2)
ZFORWARD, ZBACK, ZPROLONG = range(3)
MASS, WXY, WZ, STEP, INVERSE, COPIES, SPECTRUM, CORNERS, SIDES = range(9)


@functools.lru_cache(maxsize=None)
def constants(parts_x, parts_y, height):
    nodes, weights, derivative, basis, values = gll_tables()
    layers = height // N
    levels = layers + 1
    group = height // 4
    assert levels + 2 <= group
    eye = np.eye(N)
    diagonal = np.diag(weights)
    stiffness = derivative.T @ diagonal @ derivative

    lefts = np.concatenate(
        [
            np.kron(derivative, eye),
            np.kron(eye, derivative),
            np.kron(stiffness, diagonal) + np.kron(diagonal, stiffness),
        ],
        axis=0,
    )
    high, low, rest = thirds(lefts)
    left_exact = np.concatenate([high, high, low, low, rest], axis=1)
    high, low, rest = thirds(np.concatenate([np.kron(basis.T, basis.T), np.kron(basis, basis)]))
    left_table = np.concatenate([high, high, low, low], axis=1)

    near, far = (1.0 - nodes) / 2.0, (1.0 + nodes) / 2.0
    vertical = np.zeros((height, levels))
    for layer in range(layers):
        vertical[layer * N : layer * N + N, layer] = near
        vertical[layer * N : layer * N + N, layer + 1] = far
    cosine, eigen_z = cosine_tables(levels)
    prolong_z = vertical @ cosine
    place = np.arange(height)
    face = np.where((np.arange(N) == 0) | (np.arange(N) == N - 1), 2.0, 1.0)
    count_z = np.where((place == 0) | (place == height - 1), 1.0, np.tile(face, layers))
    grouped = np.zeros((height, 4, group))
    grouped[:, :, :levels] = prolong_z[:, None, :]
    grouped = grouped.reshape(height, height)
    many = np.eye(layers)
    rights = [np.kron(many, derivative.T), np.kron(many, stiffness)]
    high, low, rest = thirds(np.concatenate(rights, axis=1))
    right_exact = np.concatenate([high, high, low, low, rest], axis=0)
    high, low, rest = thirds(grouped)
    right_exact = np.concatenate(
        [right_exact, np.concatenate([high, high, low, low, high], axis=0)], axis=1
    )
    rights = [np.kron(many, basis), np.kron(many, basis.T), grouped.T]
    high, low, rest = thirds(np.concatenate(rights, axis=1))
    right_table = np.concatenate([high, high, low], axis=0)

    weight_xy = np.kron(weights, weights)[:, None] * np.ones((1, height))
    weight_z = np.ones((N * N, 1)) * np.tile(weights, layers)[None, :]
    mass = weight_xy * weight_z
    count_xy = np.kron(face, face)
    copies = count_xy[:, None] * count_z[None, :]
    spectrum = (values[:, None] + values[None, :]).reshape(-1)[:, None] + np.tile(values, layers)
    near_x, far_x = np.repeat(near, N), np.repeat(far, N)
    near_y, far_y = np.tile(near, N), np.tile(far, N)
    sides = np.zeros((N * N, height))
    sides[:, 0], sides[:, 1], sides[:, 2], sides[:, 3] = near_x, far_x, near_y, far_y
    corner = np.stack([near_x * near_y, near_x * far_y, far_x * near_y, far_x * far_y], axis=1)
    corners = np.repeat(corner, group, axis=1)
    plain = np.concatenate(
        [
            mass,
            weight_xy,
            weight_z,
            time_step / (mass * copies),
            1.0 / (mass * copies),
            1.0 / copies,
            1.0 / (spectrum + local_shift),
            corners,
            sides,
        ],
        axis=0,
    ).astype(np.float32)

    hartley_x, eigen_x = hartley_tables(parts_x)
    hartley_y, eigen_y = hartley_tables(parts_y)
    vertex = []
    for step_x in (0, 1):
        for step_y in (0, 1):
            vertex.append(
                np.kron(np.roll(hartley_x, -step_x, axis=1), np.roll(hartley_y, -step_y, axis=1))
            )
    modes = parts_x * parts_y
    pieces = mode_pieces(modes)
    high, low, rest = thirds(np.stack(vertex))
    vertex_table = np.stack([high, low]).reshape(8, pieces, modes // pieces, modes)
    vertex_table = vertex_table.transpose(1, 0, 2, 3).reshape(pieces, -1, modes)
    rows = np.concatenate(
        [np.repeat(hartley_x, parts_y, axis=1), np.tile(hartley_y, (1, parts_x))], axis=0
    ).astype(np.float32)
    rows = rows.reshape(parts_x + parts_y, pieces, -1).transpose(1, 0, 2)
    horizontal = (eigen_x[:, None] + eigen_y[None, :]).reshape(-1)
    inverse = np.zeros((modes, 4, group))
    inverse[:, :, :levels] = (
        1.0 / (2.0 * (horizontal[:, None] + eigen_z[None, :]) + coarse_shift)
    )[:, None, :]
    inverse = inverse.reshape(pieces, -1, height).astype(np.float32)
    return left_exact, right_exact, left_table, right_table, plain, vertex_table, rows, inverse


def split(values):
    high = values.astype(BF16)
    return high, (values - high.astype(F32)).astype(BF16)


def split_thrice(values):
    high = values.astype(BF16)
    rest = values - high.astype(F32)
    low = rest.astype(BF16)
    return high, low, (rest - low.astype(F32)).astype(BF16)


def product(first, second):
    return jnp.dot(first, second, preferred_element_type=F32)


EXCHANGES = (4, 4, 1, 1, 4, 3)
GATHERS = 3
OPERANDS = 11


def kernel(
    parts,
    *refs,
):
    operands, (state_ref, pressure_ref) = refs[:OPERANDS], refs[OPERANDS : OPERANDS + 2]
    held = refs[OPERANDS + 2 : 2 * OPERANDS + 2]
    load_sem, *scratch = refs[2 * OPERANDS + 2 :]
    loads = [
        pltpu.make_async_copy(source, here, load_sem.at[index])
        for index, (source, here) in enumerate(zip(operands, held))
    ]
    for load in loads:
        load.start()
    (
        flow_ref,
        left_exact_ref,
        right_exact_ref,
        plain_ref,
        roof_ref,
        old_ref,
        rows_ref,
        left_ref,
        right_ref,
        vertex_ref,
        modes_ref,
    ) = held

    parts_x, parts_y = parts
    devices = parts_x * parts_y
    count = len(EXCHANGES)
    fields = scratch[0:count]
    y_out = scratch[count : 2 * count]
    c_out = scratch[2 * count : 3 * count]
    x_in = scratch[3 * count : 4 * count]
    y_in = scratch[4 * count : 5 * count]
    c_in = scratch[5 * count : 6 * count]
    row_out, line, gathered, send_sem, recv_sem, *gather_sems = scratch[6 * count :]
    row_send, row_recv, line_send, line_recv = gather_sems
    height = old_ref.shape[1]
    points = old_ref.shape[0]

    my_x, my_y = lax.axis_index("gx"), lax.axis_index("gy")

    barrier = pltpu.get_barrier_semaphore()

    def others(size, mine, action):
        def one(step, carry):
            action(lax.rem(mine + step, size))
            return carry

        if size <= 8:
            for step in range(1, size):
                one(step, 0)
        else:
            lax.fori_loop(1, size, one, 0)

    def greet(other_x, other_y):
        pl.semaphore_signal(barrier, inc=1, device_id=(other_x, other_y), device_id_type=MESH)

    before_x, after_x = lax.rem(my_x + parts_x - 1, parts_x), lax.rem(my_x + 1, parts_x)
    before_y, after_y = lax.rem(my_y + parts_y - 1, parts_y), lax.rem(my_y + 1, parts_y)

    others(parts_x, my_x, lambda other: greet(other, my_y))
    others(parts_y, my_y, lambda other: greet(my_x, other))
    for corner_x in (after_x, before_x):
        for corner_y in (after_y, before_y):
            greet(corner_x, corner_y)
    greetings = parts_x - 1 + parts_y - 1 + 4

    def block(which):
        return plain_ref[which * points : (which + 1) * points, :]

    def left_exact(values, first, last):
        high, low = split(values)
        stacked = jnp.concatenate([high, low, high, low, high], axis=0)
        return product(left_exact_ref[first * points : last * points, :], stacked)

    def right_exact(values, first, last):
        high, low = split(values)
        stacked = jnp.concatenate([high, low, high, low, high], axis=1)
        return product(stacked, right_exact_ref[:, first * height : last * height])

    def left(values, first, last):
        high, low = split(values)
        stacked = jnp.concatenate([high, low, high, low], axis=0)
        return product(left_ref[first * points : last * points, :], stacked)

    def right(values, first, last):
        high, low = split(values)
        stacked = jnp.concatenate([high, low, high], axis=1)
        return product(stacked, right_ref[:, first * height : last * height])

    lane = lax.broadcasted_iota(jnp.int32, (points, height), 1)
    joins_up = (lax.rem(lane, N) == N - 1) & (lane < height - 1)
    joins_down = (lax.rem(lane, N) == 0) & (lane > 0)

    def pair_z(values):
        up = pltpu.roll(values, height - 1, 1)
        down = pltpu.roll(values, 1, 1)
        return values + jnp.where(joins_up, up, jnp.where(joins_down, down, 0.0))

    def copies(which):
        field = fields[which]
        plan = []
        x_faces = (field.at[:, points - N : points, :], field.at[:, 0:N, :])
        for side, target in ((0, after_x), (1, before_x)):
            plan.append((x_faces[side], x_in[which].at[side], (target, my_y)))
        for corner, target in enumerate(
            ((after_x, after_y), (after_x, before_y), (before_x, after_y), (before_x, before_y))
        ):
            plan.append((c_out[which].at[corner], c_in[which].at[corner], target))
        for side, target in ((0, after_y), (1, before_y)):
            plan.append((y_out[which].at[side], y_in[which].at[side], (my_x, target)))
        return [
            pltpu.make_async_remote_copy(
                src_ref=source,
                dst_ref=landing,
                send_sem=send_sem.at[which, index],
                recv_sem=recv_sem.at[which, index],
                device_id=target,
                device_id_type=MESH,
            )
            for index, (source, landing, target) in enumerate(plan)
        ]

    def stage(which, values, first=0):
        values = [pair_z(value) for value in values]
        for index, value in enumerate(values, first):
            fields[which][index] = value
            solid = value.reshape(N, N, height)
            y_out[which][0, index * N : index * N + N, :] = solid[:, N - 1, :]
            y_out[which][1, index * N : index * N + N, :] = solid[:, 0, :]
            for corner, row in enumerate((points - 1, points - N, N - 1, 0)):
                c_out[which][corner, index : index + 1, :] = value[row : row + 1, :]
        return values

    def start(which, values):
        values = stage(which, values)
        for copy in copies(which):
            copy.start()
        return values

    row_of_x = lax.broadcasted_iota(jnp.int32, (N, height), 0)

    def finish(which, values):
        for copy in copies(which):
            copy.wait_recv()
        return join(which, values)

    def join(which, values, first=0):
        results = []
        for index, value in enumerate(values, first):
            solid = value.reshape(N, N, height)
            from_x = x_in[which][:, index]
            first_y = y_in[which][0, index * N : index * N + N, :]
            last_y = y_in[which][1, index * N : index * N + N, :]
            corner = [c_in[which][which_one, index : index + 1, :] for which_one in range(4)]
            first_y = first_y + jnp.where(row_of_x == 0, corner[0], 0.0)
            last_y = last_y + jnp.where(row_of_x == 0, corner[1], 0.0)
            first_y = first_y + jnp.where(row_of_x == N - 1, corner[2], 0.0)
            last_y = last_y + jnp.where(row_of_x == N - 1, corner[3], 0.0)
            slabs = []
            for x in range(N):
                slab = solid[x]
                if x == 0:
                    slab = slab + from_x[0]
                if x == N - 1:
                    slab = slab + from_x[1]
                slab = slab + jnp.where(row_of_x == 0, first_y[x : x + 1, :], 0.0)
                slab = slab + jnp.where(row_of_x == N - 1, last_y[x : x + 1, :], 0.0)
                slabs.append(slab)
            results.append(jnp.concatenate(slabs, axis=0))
        return results

    def spread(which, row):
        row_out[which] = row
        line[which, pl.ds(my_y, 1), :] = row

        def send(other_y):
            pltpu.make_async_remote_copy(
                src_ref=row_out.at[which],
                dst_ref=line.at[which, pl.ds(my_y, 1), :],
                send_sem=row_send.at[which],
                recv_sem=row_recv.at[which],
                device_id=(my_x, other_y),
                device_id_type=MESH,
            ).start()

        others(parts_y, my_y, send)

    def line_rows(which):
        rows = line.at[which, pl.ds(0, parts_y - 1), :]
        return pltpu.make_async_remote_copy(
            src_ref=rows,
            dst_ref=rows,
            send_sem=row_send.at[which],
            recv_sem=row_recv.at[which],
            device_id=(my_x, after_y),
            device_id_type=MESH,
        )

    def relay(which):
        line_rows(which).wait_recv()
        here = pl.ds(pl.multiple_of(my_x * parts_y, parts_y), parts_y)
        gathered[which, here, :] = line[which]

        def send(other_x):
            pltpu.make_async_remote_copy(
                src_ref=line.at[which],
                dst_ref=gathered.at[which, here, :],
                send_sem=line_send.at[which],
                recv_sem=line_recv.at[which],
                device_id=(other_x, my_y),
                device_id_type=MESH,
            ).start()

        others(parts_x, my_x, send)

    def all_lines(which):
        rows = gathered.at[which, pl.ds(0, devices - parts_y), :]
        return pltpu.make_async_remote_copy(
            src_ref=rows,
            dst_ref=rows,
            send_sem=line_send.at[which],
            recv_sem=line_recv.at[which],
            device_id=(after_x, my_y),
            device_id_type=MESH,
        )

    def collect(which):
        all_lines(which).wait_recv()
        return gathered[which]

    one_row = lax.broadcasted_iota(jnp.int32, (1, height), 1)
    group = height // 4
    spare = height // N + 1

    def operate(values):
        xy = left_exact(values, DX, KXY + 1)
        z = right_exact(values, ZD, ZK + 1)
        image = xy[2 * points :] * weight_z + weight_xy * z[:, height:]
        gradient = [mass * xy[:points], mass * xy[points : 2 * points], mass * z[:, :height]]
        return image + helmholtz_shift * mass * values, gradient

    def coarse_row(part):
        high, low, rest = split_thrice(part)
        stacked = jnp.concatenate([high, low, high, low, rest], axis=1)
        table = right_exact_ref[:, ZRESTRICT * height : (ZRESTRICT + 1) * height]
        terms = block(CORNERS) * product(stacked, table)
        return jnp.sum(terms, axis=0, keepdims=True)

    def with_scalars(row, residual, smoothed, image):
        gamma = jnp.sum(residual * smoothed * block(COPIES), axis=0, keepdims=True)
        delta = jnp.sum(smoothed * image, axis=0, keepdims=True)
        gamma = jnp.sum(gamma, axis=1, keepdims=True)
        delta = jnp.sum(delta, axis=1, keepdims=True)
        return jnp.where(one_row == spare, gamma, jnp.where(one_row == spare + 1, delta, row))

    def scalars(rows):
        total = jnp.sum(rows, axis=0, keepdims=True)
        return total[:, spare : spare + 1], total[:, spare + 1 : spare + 2]

    def local_solve(residual):
        modal = right(left(residual, FORWARD, FORWARD + 1), ZFORWARD, ZFORWARD + 1)
        modal = modal * block(SPECTRUM)
        return left(right(modal, ZBACK, ZBACK + 1), BACK, BACK + 1)

    def own_modes(piece):
        sides = block(SIDES)
        next_x, next_y = lax.rem(my_x + 1, parts_x), lax.rem(my_y + 1, parts_y)

        def row(which):
            return rows_ref[piece, pl.ds(which, 1), :]

        own_x = sides[:, 0:1] * row(my_x) + sides[:, 1:2] * row(next_x)
        own_y = sides[:, 2:3] * row(parts_x + my_y) + sides[:, 3:4] * row(parts_x + next_y)
        return split(own_x * own_y)

    pieces = modes_ref.shape[0]
    length = modes_ref.shape[1]
    span = length if pieces == 1 else 2 * length
    mode_lane = lax.broadcasted_iota(jnp.int32, (length, height), 1)

    def coarse_piece(piece, stacked, own):
        each = product(vertex_ref[piece, :, :span], stacked[:span])
        for begin in range(span, devices, span):
            lines = slice(begin, begin + span)
            each = each + product(vertex_ref[piece, :, lines], stacked[lines])
        tops, lows = each[: 4 * length], each[4 * length :]
        each = (tops[:, 2 * height :] + lows[:, height : 2 * height]) + (
            tops[:, height : 2 * height] + lows[:, :height]
        )
        each = each + tops[:, :height]
        total = jnp.zeros((length, height), F32)
        for corner in range(4):
            chosen = (mode_lane >= corner * group) & (mode_lane < corner * group + group)
            total = jnp.where(chosen, each[corner * length : (corner + 1) * length], total)
        levels = right(total * modes_ref[piece], ZPROLONG, ZPROLONG + 1)
        high, low = split(levels)
        own_high, own_low = own
        return product(own_high, high) + (product(own_high, low) + product(own_low, high))

    def coarse_solve(rows):
        stacked = jnp.concatenate(split_thrice(rows), axis=1)
        if pieces == 1:
            return coarse_piece(0, stacked, own)
        total = jnp.zeros((points, height), F32)
        for piece in range(pieces):
            total = total + coarse_piece(piece, stacked, own_modes(piece))
        return total

    for load in loads[:5]:
        load.wait()
    mass, weight_xy, weight_z = block(MASS), block(WXY), block(WZ)
    flow = [flow_ref[part * points : (part + 1) * points, :] for part in range(4)]
    u, v, w, theta = flow
    xy = left_exact(jnp.concatenate(flow, axis=1), DX, KXY + 1)
    z = right_exact(flow_ref[...], ZD, ZK + 1)
    canopy = jnp.where(lane // N < roof_ref[...], 1.0, 0.0)
    drag = drag_strength * canopy * jnp.sqrt(u * u + v * v + w * w)
    forcing = [-drag * u, -drag * v, -drag * w + buoyancy * theta, heating * canopy]
    rates = []
    for part in range(4):
        lanes = slice(part * height, (part + 1) * height)
        rows = slice(part * points, (part + 1) * points)
        advection = u * xy[:points, lanes] + v * xy[points : 2 * points, lanes] + w * z[rows, :height]
        friction = xy[2 * points :, lanes] * weight_z + weight_xy * z[rows, height:]
        rates.append(mass * (forcing[part] - advection) - viscosity * friction)
    pl.semaphore_wait(barrier, greetings)
    rates = start(0, rates)

    for load in loads[5:]:
        load.wait()
    old = old_ref[...]
    old_image, old_gradient = operate(old)
    old_gradient = stage(1, old_gradient, 1)
    own = own_modes(0) if pieces == 1 else None

    rates = finish(0, rates)
    step = block(STEP)
    provisional = [values + step * rate for values, rate in zip(flow, rates)]
    provisional[2] = jnp.where((lane == 0) | (lane == height - 1), 0.0, provisional[2])
    divergence = (
        left_exact(provisional[0], DX, DX + 1)
        + left_exact(provisional[1], DY, DY + 1)
        + right_exact(provisional[2], ZD, ZD + 1)
    )
    raw = -mass * divergence - old_image
    whole = start(1, [raw])
    spread(0, coarse_row(raw))
    residual = finish(1, whole)[0]
    relay(0)

    local = start(2, [local_solve(residual)])
    coarse = coarse_solve(collect(0))
    first = finish(2, local)[0] + coarse
    raw, first_gradient = operate(first)
    image = start(3, [raw])
    spread(1, with_scalars(coarse_row(raw), residual, first, raw))
    first_gradient = stage(4, first_gradient, 1)
    image = finish(3, image)[0]
    relay(1)

    local = start(4, [local_solve(image)])
    rows = collect(1)
    coarse = coarse_solve(rows)
    gamma_first, delta_first = scalars(rows)
    alpha_first = gamma_first / delta_first
    residual = residual - alpha_first * image
    second = first - alpha_first * (finish(4, local)[0] + coarse)
    raw, second_gradient = operate(second)
    spread(2, with_scalars(jnp.zeros((1, height), F32), residual, second, raw))
    second_gradient = start(5, second_gradient)
    relay(2)
    gradients = join(1, old_gradient, 1) + join(4, first_gradient, 1)
    gamma, delta = scalars(collect(2))
    ratio = gamma / gamma_first
    alpha = gamma / (delta - ratio * gamma / alpha_first)
    weight_first = alpha_first + alpha * ratio
    pressure_ref[...] = old + weight_first * first + alpha * second
    state_ref[3 * points : 4 * points, :] = provisional[3]
    second_gradient = finish(5, second_gradient)
    inverse = block(INVERSE)
    for part in range(3):
        total = gradients[part] + weight_first * gradients[3 + part] + alpha * second_gradient[part]
        state_ref[part * points : (part + 1) * points, :] = provisional[part] - total * inverse

    for which in range(count):
        for copy in copies(which):
            copy.wait_send()
    for which in range(GATHERS):
        line_rows(which).wait_send()
        all_lines(which).wait_send()


def on_device(flow_state, building_height, pressure_old):
    parts = (lax.axis_size("gx"), lax.axis_size("gy"))
    devices = parts[0] * parts[1]
    components, width, depth, height = flow_state.shape
    points = width * depth
    assert width == N and depth == N and components == 4
    tables = constants(parts[0], parts[1], height)
    left_exact, right_exact, left, right, plain, vertex, rows, modes = [
        jnp.asarray(table) for table in tables
    ]
    operands = [
        flow_state.reshape(components * points, height),
        left_exact,
        right_exact,
        plain,
        building_height,
        pressure_old.reshape(points, height),
        rows,
        left,
        right,
        vertex,
        modes,
    ]
    scratch = [pltpu.VMEM(operand.shape, operand.dtype) for operand in operands]
    scratch += [pltpu.SemaphoreType.DMA((len(operands),))]
    scratch += [pltpu.VMEM((number, points, height), F32) for number in EXCHANGES]
    scratch += [pltpu.VMEM((2, number * N, height), F32) for number in EXCHANGES]
    scratch += [pltpu.VMEM((4, number, height), F32) for number in EXCHANGES]
    scratch += [pltpu.VMEM((2, number, N, height), F32) for number in EXCHANGES]
    scratch += [pltpu.VMEM((2, number * N, height), F32) for number in EXCHANGES]
    scratch += [pltpu.VMEM((4, number, height), F32) for number in EXCHANGES]
    scratch += [
        pltpu.VMEM((GATHERS, 1, height), F32),
        pltpu.VMEM((GATHERS, parts[1], height), F32),
        pltpu.VMEM((GATHERS, devices, height), F32),
        pltpu.SemaphoreType.DMA((len(EXCHANGES), 8)),
        pltpu.SemaphoreType.DMA((len(EXCHANGES), 8)),
        pltpu.SemaphoreType.DMA((GATHERS,)),
        pltpu.SemaphoreType.DMA((GATHERS,)),
        pltpu.SemaphoreType.DMA((GATHERS,)),
        pltpu.SemaphoreType.DMA((GATHERS,)),
    ]
    whole = pl.BlockSpec(memory_space=pltpu.VMEM)
    state, pressure = pl.pallas_call(
        functools.partial(kernel, parts),
        out_shape=(
            pltpu.VMEM((components * points, height), F32),
            pltpu.VMEM((points, height), F32),
        ),
        in_specs=[pl.BlockSpec(memory_space=pltpu.HBM)] * len(operands),
        out_specs=(whole, whole),
        scratch_shapes=scratch,
        compiler_params=pltpu.CompilerParams(
            collective_id=0, has_side_effects=True, vmem_limit_bytes=60 * 2**20
        ),
    )(*operands)
    return state.reshape(flow_state.shape), pressure.reshape(pressure_old.shape)


def solution(mesh):
    in_specs = (P(None, "gx", "gy", None), P("gx", "gy"), P("gx", "gy", None))
    out_specs = (P(None, "gx", "gy", None), P("gx", "gy", None))
    return jax.shard_map(
        on_device, mesh=mesh, in_specs=in_specs, out_specs=out_specs, check_vma=False
    )
```

```python
import functools
import math

import jax
import jax.numpy as jnp
import ml_dtypes
import numpy as np
from jax import lax
from jax.experimental import pallas as pl
from jax.experimental.pallas import tpu as pltpu
from jax.sharding import PartitionSpec as P

F32 = jnp.float32
BF16 = jnp.bfloat16
MESH = pl.DeviceIdType.MESH
N = 8
viscosity = 0.05
time_step = 0.01
drag_strength = 20.0
heating = 40.0
buoyancy = 10.0
helmholtz_shift = 0.001
local_shift = 0.5
coarse_shift = 0.02
gll_points = (
    -1.0,
    -0.8717401485096066,
    -0.5917001814331423,
    -0.2092992179024789,
    0.2092992179024789,
    0.5917001814331423,
    0.8717401485096066,
    1.0,
)


def legendre_seven(points):
    squared = points * points
    return points * (((429.0 * squared - 693.0) * squared + 315.0) * squared - 35.0) / 16.0


def jacobi_eigen(matrix):
    current = np.array(matrix)
    basis = np.eye(8)
    for rounds in range(12):
        for first in range(7):
            for second in range(first + 1, 8):
                rotation_angle = 0.5 * math.atan2(
                    2.0 * float(current[first, second]),
                    float(current[second, second] - current[first, first]),
                )
                cosine = math.cos(rotation_angle)
                sine = math.sin(rotation_angle)
                rotation = np.eye(8)
                rotation[first, first] = cosine
                rotation[second, second] = cosine
                rotation[first, second] = sine
                rotation[second, first] = -sine
                current = rotation.T @ current @ rotation
                basis = basis @ rotation
    return (np.sum(current * np.eye(8), axis=0), basis)


def gll_tables():
    gll_nodes = np.array(gll_points)
    values = legendre_seven(gll_nodes)
    weights = 2.0 / (56.0 * values * values)
    differ = gll_nodes[:, None] - gll_nodes[None, :] + np.eye(8)
    derivative = values[:, None] / values[None, :] / differ * (1.0 - np.eye(8))
    derivative = (
        derivative + np.eye(8) * np.array([-14.0, 0.0, 0.0, 0.0, 0.0, 0.0, 0.0, 14.0])[None, :]
    )
    stiffness = derivative.T @ (weights[:, None] * derivative)
    scaled = stiffness / np.sqrt(np.outer(weights, weights))
    scaled = 0.5 * (scaled + scaled.T)
    eigen_values, eigen_vectors = jacobi_eigen(scaled)
    eigen_basis = eigen_vectors / np.sqrt(weights)[:, None]
    return (gll_nodes, weights, derivative, eigen_basis, np.maximum(eigen_values, 0.0))


def hartley_tables(count):
    index = np.arange(count)
    angle = 2.0 * np.pi / count * (index[:, None] * index[None, :] % count)
    hartley = (np.cos(angle) + np.sin(angle)) / np.sqrt(count)
    return hartley, 2.0 - 2.0 * np.cos(2.0 * np.pi / count * index)


def cosine_tables(count):
    index = np.arange(count)
    angle = np.pi / count * (index[:, None] + 0.5) * index[None, :]
    norms = np.where(index == 0, np.sqrt(1.0 / count), np.sqrt(2.0 / count))
    return np.cos(angle) * norms[None, :], 2.0 - 2.0 * np.cos(np.pi / count * index)


def thirds(matrix):
    pieces = []
    for piece in range(3):
        pieces.append(matrix.astype(np.float32).astype(ml_dtypes.bfloat16))
        matrix = matrix - pieces[-1].astype(np.float64)
    return pieces


def mode_pieces(modes):
    return modes // 128 if modes > 128 and modes % 128 == 0 else 1


DX, DY, KXY = range(3)
ZD, ZK, ZRESTRICT = range(3)
FORWARD, BACK = range(2)
ZFORWARD, ZBACK, ZPROLONG = range(3)
MASS, WXY, WZ, STEP, INVERSE, COPIES, SPECTRUM, CORNERS, SIDES = range(9)


@functools.lru_cache(maxsize=None)
def constants(parts_x, parts_y, height):
    nodes, weights, derivative, basis, values = gll_tables()
    layers = height // N
    levels = layers + 1
    group = height // 4
    assert levels + 2 <= group
    eye = np.eye(N)
    diagonal = np.diag(weights)
    stiffness = derivative.T @ diagonal @ derivative

    lefts = np.concatenate(
        [
            np.kron(derivative, eye),
            np.kron(eye, derivative),
            np.kron(stiffness, diagonal) + np.kron(diagonal, stiffness),
        ],
        axis=0,
    )
    high, low, rest = thirds(lefts)
    left_exact = np.concatenate([high, high, low, low, rest], axis=1)
    high, low, rest = thirds(np.concatenate([np.kron(basis.T, basis.T), np.kron(basis, basis)]))
    left_table = np.concatenate([high, high, low, low], axis=1)

    near, far = (1.0 - nodes) / 2.0, (1.0 + nodes) / 2.0
    vertical = np.zeros((height, levels))
    for layer in range(layers):
        vertical[layer * N : layer * N + N, layer] = near
        vertical[layer * N : layer * N + N, layer + 1] = far
    cosine, eigen_z = cosine_tables(levels)
    prolong_z = vertical @ cosine
    place = np.arange(height)
    face = np.where((np.arange(N) == 0) | (np.arange(N) == N - 1), 2.0, 1.0)
    count_z = np.where((place == 0) | (place == height - 1), 1.0, np.tile(face, layers))
    grouped = np.zeros((height, 4, group))
    grouped[:, :, :levels] = prolong_z[:, None, :]
    grouped = grouped.reshape(height, height)
    many = np.eye(layers)
    rights = [np.kron(many, derivative.T), np.kron(many, stiffness)]
    high, low, rest = thirds(np.concatenate(rights, axis=1))
    right_exact = np.concatenate([high, high, low, low, rest], axis=0)
    high, low, rest = thirds(grouped)
    right_exact = np.concatenate(
        [right_exact, np.concatenate([high, high, low, low, high], axis=0)], axis=1
    )
    rights = [np.kron(many, basis), np.kron(many, basis.T), grouped.T]
    high, low, rest = thirds(np.concatenate(rights, axis=1))
    right_table = np.concatenate([high, high, low], axis=0)

    weight_xy = np.kron(weights, weights)[:, None] * np.ones((1, height))
    weight_z = np.ones((N * N, 1)) * np.tile(weights, layers)[None, :]
    mass = weight_xy * weight_z
    count_xy = np.kron(face, face)
    copies = count_xy[:, None] * count_z[None, :]
    spectrum = (values[:, None] + values[None, :]).reshape(-1)[:, None] + np.tile(values, layers)
    near_x, far_x = np.repeat(near, N), np.repeat(far, N)
    near_y, far_y = np.tile(near, N), np.tile(far, N)
    sides = np.zeros((N * N, height))
    sides[:, 0], sides[:, 1], sides[:, 2], sides[:, 3] = near_x, far_x, near_y, far_y
    corner = np.stack([near_x * near_y, near_x * far_y, far_x * near_y, far_x * far_y], axis=1)
    corners = np.repeat(corner, group, axis=1)
    plain = np.concatenate(
        [
            mass,
            weight_xy,
            weight_z,
            time_step / (mass * copies),
            1.0 / (mass * copies),
            1.0 / copies,
            1.0 / (spectrum + local_shift),
            corners,
            sides,
        ],
        axis=0,
    ).astype(np.float32)

    hartley_x, eigen_x = hartley_tables(parts_x)
    hartley_y, eigen_y = hartley_tables(parts_y)
    vertex = []
    for step_x in (0, 1):
        for step_y in (0, 1):
            vertex.append(
                np.kron(np.roll(hartley_x, -step_x, axis=1), np.roll(hartley_y, -step_y, axis=1))
            )
    modes = parts_x * parts_y
    pieces = mode_pieces(modes)
    high, low, rest = thirds(np.stack(vertex))
    vertex_table = np.stack([high, low]).reshape(8, pieces, modes // pieces, modes)
    vertex_table = vertex_table.transpose(1, 0, 2, 3).reshape(pieces, -1, modes)
    rows = np.concatenate(
        [np.repeat(hartley_x, parts_y, axis=1), np.tile(hartley_y, (1, parts_x))], axis=0
    ).astype(np.float32)
    rows = rows.reshape(parts_x + parts_y, pieces, -1).transpose(1, 0, 2)
    horizontal = (eigen_x[:, None] + eigen_y[None, :]).reshape(-1)
    inverse = np.zeros((modes, 4, group))
    inverse[:, :, :levels] = (
        1.0 / (2.0 * (horizontal[:, None] + eigen_z[None, :]) + coarse_shift)
    )[:, None, :]
    inverse = inverse.reshape(pieces, -1, height).astype(np.float32)
    return left_exact, right_exact, left_table, right_table, plain, vertex_table, rows, inverse


def split(values):
    high = values.astype(BF16)
    return high, (values - high.astype(F32)).astype(BF16)


def split_thrice(values):
    high = values.astype(BF16)
    rest = values - high.astype(F32)
    low = rest.astype(BF16)
    return high, low, (rest - low.astype(F32)).astype(BF16)


def product(first, second):
    return jnp.dot(first, second, preferred_element_type=F32)


EXCHANGES = (4, 4, 1, 1, 4, 3)
GATHERS = 3
OPERANDS = 11


def kernel(
    parts,
    *refs,
):
    operands, (state_ref, pressure_ref) = refs[:OPERANDS], refs[OPERANDS : OPERANDS + 2]
    held = refs[OPERANDS + 2 : 2 * OPERANDS + 2]
    load_sem, *scratch = refs[2 * OPERANDS + 2 :]
    loads = [
        pltpu.make_async_copy(source, here, load_sem.at[index])
        for index, (source, here) in enumerate(zip(operands, held))
    ]
    for load in loads:
        load.start()
    (
        flow_ref,
        left_exact_ref,
        right_exact_ref,
        plain_ref,
        roof_ref,
        old_ref,
        rows_ref,
        left_ref,
        right_ref,
        vertex_ref,
        modes_ref,
    ) = held

    parts_x, parts_y = parts
    devices = parts_x * parts_y
    count = len(EXCHANGES)
    fields = scratch[0:count]
    y_out = scratch[count : 2 * count]
    c_out = scratch[2 * count : 3 * count]
    x_in = scratch[3 * count : 4 * count]
    y_in = scratch[4 * count : 5 * count]
    c_in = scratch[5 * count : 6 * count]
    row_out, gathered, send_sem, recv_sem, row_send, row_recv = scratch[6 * count :]
    height = old_ref.shape[1]
    points = old_ref.shape[0]

    my_x, my_y = lax.axis_index("gx"), lax.axis_index("gy")
    me = my_x * parts_y + my_y

    barrier = pltpu.get_barrier_semaphore()

    def each_other(action):
        if devices <= 64:
            all_x = [lax.rem(my_x + step, parts_x) for step in range(parts_x)]
            all_y = [lax.rem(my_y + step, parts_y) for step in range(parts_y)]
            for step in range(1, devices):
                action(all_x[step // parts_y], all_y[step % parts_y])
            return

        def one(step, carry):
            other = lax.rem(me + step, devices)
            action(other // parts_y, lax.rem(other, parts_y))
            return carry

        lax.fori_loop(1, devices, one, 0)

    def greet(other_x, other_y):
        pl.semaphore_signal(barrier, inc=1, device_id=(other_x, other_y), device_id_type=MESH)

    each_other(greet)

    before_x, after_x = lax.rem(my_x + parts_x - 1, parts_x), lax.rem(my_x + 1, parts_x)
    before_y, after_y = lax.rem(my_y + parts_y - 1, parts_y), lax.rem(my_y + 1, parts_y)

    def block(which):
        return plain_ref[which * points : (which + 1) * points, :]

    def left_exact(values, first, last):
        high, low = split(values)
        stacked = jnp.concatenate([high, low, high, low, high], axis=0)
        return product(left_exact_ref[first * points : last * points, :], stacked)

    def right_exact(values, first, last):
        high, low = split(values)
        stacked = jnp.concatenate([high, low, high, low, high], axis=1)
        return product(stacked, right_exact_ref[:, first * height : last * height])

    def left(values, first, last):
        high, low = split(values)
        stacked = jnp.concatenate([high, low, high, low], axis=0)
        return product(left_ref[first * points : last * points, :], stacked)

    def right(values, first, last):
        high, low = split(values)
        stacked = jnp.concatenate([high, low, high], axis=1)
        return product(stacked, right_ref[:, first * height : last * height])

    lane = lax.broadcasted_iota(jnp.int32, (points, height), 1)
    joins_up = ((lane & (N - 1)) == N - 1) & (lane < height - 1)
    joins_down = ((lane & (N - 1)) == 0) & (lane > 0)

    def pair_z(values):
        up = pltpu.roll(values, height - 1, 1)
        down = pltpu.roll(values, 1, 1)
        return values + jnp.where(joins_up, up, jnp.where(joins_down, down, 0.0))

    def copies(which):
        field = fields[which]
        plan = []
        x_faces = (field.at[:, points - N : points, :], field.at[:, 0:N, :])
        for side, target in ((0, after_x), (1, before_x)):
            plan.append((x_faces[side], x_in[which].at[side], (target, my_y)))
        for corner, target in enumerate(
            ((after_x, after_y), (after_x, before_y), (before_x, after_y), (before_x, before_y))
        ):
            plan.append((c_out[which].at[corner], c_in[which].at[corner], target))
        for side, target in ((0, after_y), (1, before_y)):
            plan.append((y_out[which].at[side], y_in[which].at[side], (my_x, target)))
        return [
            pltpu.make_async_remote_copy(
                src_ref=source,
                dst_ref=landing,
                send_sem=send_sem.at[which, index],
                recv_sem=recv_sem.at[which, index],
                device_id=target,
                device_id_type=MESH,
            )
            for index, (source, landing, target) in enumerate(plan)
        ]

    def stage(which, values, first=0):
        values = [pair_z(value) for value in values]
        for index, value in enumerate(values, first):
            fields[which][index] = value
            solid = value.reshape(N, N, height)
            y_out[which][0, index * N : index * N + N, :] = solid[:, N - 1, :]
            y_out[which][1, index * N : index * N + N, :] = solid[:, 0, :]
            for corner, row in enumerate((points - 1, points - N, N - 1, 0)):
                c_out[which][corner, index : index + 1, :] = value[row : row + 1, :]
        return values

    def start(which, values):
        values = stage(which, values)
        for copy in copies(which):
            copy.start()
        return values

    row_of_x = lax.broadcasted_iota(jnp.int32, (N, height), 0)

    def finish(which, values):
        for copy in copies(which):
            copy.wait_recv()
        return join(which, values)

    def join(which, values, first=0):
        results = []
        for index, value in enumerate(values, first):
            solid = value.reshape(N, N, height)
            from_x = x_in[which][:, index]
            first_y = y_in[which][0, index * N : index * N + N, :]
            last_y = y_in[which][1, index * N : index * N + N, :]
            corner = [c_in[which][which_one, index : index + 1, :] for which_one in range(4)]
            first_y = first_y + jnp.where(row_of_x == 0, corner[0], 0.0)
            last_y = last_y + jnp.where(row_of_x == 0, corner[1], 0.0)
            first_y = first_y + jnp.where(row_of_x == N - 1, corner[2], 0.0)
            last_y = last_y + jnp.where(row_of_x == N - 1, corner[3], 0.0)
            slabs = []
            for x in range(N):
                slab = solid[x]
                if x == 0:
                    slab = slab + from_x[0]
                if x == N - 1:
                    slab = slab + from_x[1]
                slab = slab + jnp.where(row_of_x == 0, first_y[x : x + 1, :], 0.0)
                slab = slab + jnp.where(row_of_x == N - 1, last_y[x : x + 1, :], 0.0)
                slabs.append(slab)
            results.append(jnp.concatenate(slabs, axis=0))
        return results

    def spread(which, row):
        row_out[which] = row
        gathered[which, pl.ds(me, 1), :] = row

        def send(other_x, other_y):
            pltpu.make_async_remote_copy(
                src_ref=row_out.at[which],
                dst_ref=gathered.at[which, pl.ds(me, 1), :],
                send_sem=row_send.at[which],
                recv_sem=row_recv.at[which],
                device_id=(other_x, other_y),
                device_id_type=MESH,
            ).start()

        each_other(send)

    def all_rows(which):
        return pltpu.make_async_remote_copy(
            src_ref=gathered.at[which, pl.ds(0, devices - 1), :],
            dst_ref=gathered.at[which, pl.ds(0, devices - 1), :],
            send_sem=row_send.at[which],
            recv_sem=row_recv.at[which],
            device_id=(after_x, my_y),
            device_id_type=MESH,
        )

    def collect(which):
        all_rows(which).wait_recv()
        return gathered[which]

    one_row = lax.broadcasted_iota(jnp.int32, (1, height), 1)
    group = height // 4
    spare = height // N + 1

    def operate(values):
        image = left_exact(values, KXY, KXY + 1) * weight_z
        image = image + weight_xy * right_exact(values, ZK, ZK + 1)
        return image + helmholtz_shift * mass * values

    def gradient(values):
        xy = left_exact(values, DX, DY + 1)
        z = right_exact(values, ZD, ZD + 1)
        return [mass * xy[:points], mass * xy[points:], mass * z]

    def coarse_row(part):
        high, low, rest = split_thrice(part)
        stacked = jnp.concatenate([high, low, high, low, rest], axis=1)
        table = right_exact_ref[:, ZRESTRICT * height : (ZRESTRICT + 1) * height]
        terms = block(CORNERS) * product(stacked, table)
        return jnp.sum(terms, axis=0, keepdims=True)

    def with_scalars(row, residual, smoothed, image):
        gamma = jnp.sum(residual * smoothed * block(COPIES), axis=0, keepdims=True)
        delta = jnp.sum(smoothed * image, axis=0, keepdims=True)
        gamma = jnp.sum(gamma, axis=1, keepdims=True)
        delta = jnp.sum(delta, axis=1, keepdims=True)
        return jnp.where(one_row == spare, gamma, jnp.where(one_row == spare + 1, delta, row))

    def scalars(rows):
        total = jnp.sum(rows, axis=0, keepdims=True)
        return total[:, spare : spare + 1], total[:, spare + 1 : spare + 2]

    def local_solve(residual):
        modal = right(left(residual, FORWARD, FORWARD + 1), ZFORWARD, ZFORWARD + 1)
        modal = modal * block(SPECTRUM)
        return left(right(modal, ZBACK, ZBACK + 1), BACK, BACK + 1)

    def own_modes(piece):
        sides = block(SIDES)
        next_x, next_y = lax.rem(my_x + 1, parts_x), lax.rem(my_y + 1, parts_y)

        def row(which):
            return rows_ref[piece, pl.ds(which, 1), :]

        own_x = sides[:, 0:1] * row(my_x) + sides[:, 1:2] * row(next_x)
        own_y = sides[:, 2:3] * row(parts_x + my_y) + sides[:, 3:4] * row(parts_x + next_y)
        return split(own_x * own_y)

    pieces = modes_ref.shape[0]
    length = modes_ref.shape[1]
    span = length if pieces == 1 else 2 * length
    mode_lane = lax.broadcasted_iota(jnp.int32, (length, height), 1)

    def coarse_piece(piece, stacked, own):
        each = product(vertex_ref[piece, :, :span], stacked[:span])
        for begin in range(span, devices, span):
            lines = slice(begin, begin + span)
            each = each + product(vertex_ref[piece, :, lines], stacked[lines])
        tops, lows = each[: 4 * length], each[4 * length :]
        each = (tops[:, 2 * height :] + lows[:, height : 2 * height]) + (
            tops[:, height : 2 * height] + lows[:, :height]
        )
        each = each + tops[:, :height]
        total = jnp.zeros((length, height), F32)
        for corner in range(4):
            chosen = (mode_lane >= corner * group) & (mode_lane < corner * group + group)
            total = jnp.where(chosen, each[corner * length : (corner + 1) * length], total)
        levels = right(total * modes_ref[piece], ZPROLONG, ZPROLONG + 1)
        high, low = split(levels)
        own_high, own_low = own
        return product(own_high, high) + (product(own_high, low) + product(own_low, high))

    def coarse_solve(rows):
        stacked = jnp.concatenate(split_thrice(rows), axis=1)
        if pieces == 1:
            return coarse_piece(0, stacked, own)
        total = jnp.zeros((points, height), F32)
        for piece in range(pieces):
            total = total + coarse_piece(piece, stacked, own_modes(piece))
        return total

    for load in loads[:5]:
        load.wait()
    mass, weight_xy, weight_z = block(MASS), block(WXY), block(WZ)
    flow = [flow_ref[part * points : (part + 1) * points, :] for part in range(4)]
    u, v, w, theta = flow
    xy = left_exact(jnp.concatenate(flow, axis=1), DX, KXY + 1)
    z = right_exact(flow_ref[...], ZD, ZK + 1)
    canopy = jnp.where(lane < N * roof_ref[...], 1.0, 0.0)
    drag = drag_strength * canopy * jnp.sqrt(u * u + v * v + w * w)
    forcing = [-drag * u, -drag * v, -drag * w + buoyancy * theta, heating * canopy]
    rates = []
    for part in range(4):
        lanes = slice(part * height, (part + 1) * height)
        rows = slice(part * points, (part + 1) * points)
        advection = u * xy[:points, lanes] + v * xy[points : 2 * points, lanes] + w * z[rows, :height]
        friction = xy[2 * points :, lanes] * weight_z + weight_xy * z[rows, height:]
        rates.append(mass * (forcing[part] - advection) - viscosity * friction)
    pl.semaphore_wait(barrier, devices - 1)
    rates = start(0, rates)

    for load in loads[5:]:
        load.wait()
    old = old_ref[...]
    old_image = operate(old)
    old_gradient = stage(1, gradient(old), 1)
    own = own_modes(0) if pieces == 1 else None

    rates = finish(0, rates)
    step = block(STEP)
    provisional = [values + step * rate for values, rate in zip(flow, rates)]
    provisional[2] = jnp.where((lane == 0) | (lane == height - 1), 0.0, provisional[2])
    divergence = (
        left_exact(provisional[0], DX, DX + 1)
        + left_exact(provisional[1], DY, DY + 1)
        + right_exact(provisional[2], ZD, ZD + 1)
    )
    raw = -mass * divergence - old_image
    whole = start(1, [raw])
    spread(0, coarse_row(raw))
    residual = finish(1, whole)[0]

    local = start(2, [local_solve(residual)])
    coarse = coarse_solve(collect(0))
    first = finish(2, local)[0] + coarse
    raw = operate(first)
    image = start(3, [raw])
    spread(1, with_scalars(coarse_row(raw), residual, first, raw))
    first_gradient = stage(4, gradient(first), 1)
    image = finish(3, image)[0]

    local = start(4, [local_solve(image)])
    rows = collect(1)
    coarse = coarse_solve(rows)
    gamma_first, delta_first = scalars(rows)
    alpha_first = gamma_first / delta_first
    residual = residual - alpha_first * image
    second = first - alpha_first * (finish(4, local)[0] + coarse)
    raw = operate(second)
    spread(2, with_scalars(jnp.zeros((1, height), F32), residual, second, raw))
    second_gradient = start(5, gradient(second))
    gradients = join(1, old_gradient, 1) + join(4, first_gradient, 1)
    gamma, delta = scalars(collect(2))
    ratio = gamma / gamma_first
    alpha = gamma / (delta - ratio * gamma / alpha_first)
    weight_first = alpha_first + alpha * ratio
    pressure_ref[...] = old + weight_first * first + alpha * second
    state_ref[3 * points : 4 * points, :] = provisional[3]
    second_gradient = finish(5, second_gradient)
    inverse = block(INVERSE)
    for part in range(3):
        total = gradients[part] + weight_first * gradients[3 + part] + alpha * second_gradient[part]
        state_ref[part * points : (part + 1) * points, :] = provisional[part] - total * inverse

    for which in range(count):
        for copy in copies(which):
            copy.wait_send()
    for which in range(GATHERS):
        all_rows(which).wait_send()


def on_device(flow_state, building_height, pressure_old):
    parts = (lax.axis_size("gx"), lax.axis_size("gy"))
    devices = parts[0] * parts[1]
    components, width, depth, height = flow_state.shape
    points = width * depth
    assert width == N and depth == N and components == 4
    tables = constants(parts[0], parts[1], height)
    left_exact, right_exact, left, right, plain, vertex, rows, modes = [
        jnp.asarray(table) for table in tables
    ]
    operands = [
        flow_state.reshape(components * points, height),
        left_exact,
        right_exact,
        plain,
        building_height,
        pressure_old.reshape(points, height),
        rows,
        left,
        right,
        vertex,
        modes,
    ]
    scratch = [pltpu.VMEM(operand.shape, operand.dtype) for operand in operands]
    scratch += [pltpu.SemaphoreType.DMA((len(operands),))]
    scratch += [pltpu.VMEM((number, points, height), F32) for number in EXCHANGES]
    scratch += [pltpu.VMEM((2, number * N, height), F32) for number in EXCHANGES]
    scratch += [pltpu.VMEM((4, number, height), F32) for number in EXCHANGES]
    scratch += [pltpu.VMEM((2, number, N, height), F32) for number in EXCHANGES]
    scratch += [pltpu.VMEM((2, number * N, height), F32) for number in EXCHANGES]
    scratch += [pltpu.VMEM((4, number, height), F32) for number in EXCHANGES]
    scratch += [
        pltpu.VMEM((GATHERS, 1, height), F32),
        pltpu.VMEM((GATHERS, devices, height), F32),
        pltpu.SemaphoreType.DMA((len(EXCHANGES), 8)),
        pltpu.SemaphoreType.DMA((len(EXCHANGES), 8)),
        pltpu.SemaphoreType.DMA((GATHERS,)),
        pltpu.SemaphoreType.DMA((GATHERS,)),
    ]
    whole = pl.BlockSpec(memory_space=pltpu.VMEM)
    state, pressure = pl.pallas_call(
        functools.partial(kernel, parts),
        out_shape=(
            pltpu.VMEM((components * points, height), F32),
            pltpu.VMEM((points, height), F32),
        ),
        in_specs=[pl.BlockSpec(memory_space=pltpu.HBM)] * len(operands),
        out_specs=(whole, whole),
        scratch_shapes=scratch,
        compiler_params=pltpu.CompilerParams(
            collective_id=0, has_side_effects=True, vmem_limit_bytes=60 * 2**20
        ),
    )(*operands)
    return state.reshape(flow_state.shape), pressure.reshape(pressure_old.shape)


def solution(mesh):
    in_specs = (P(None, "gx", "gy", None), P("gx", "gy"), P("gx", "gy", None))
    out_specs = (P(None, "gx", "gy", None), P("gx", "gy", None))
    return jax.shard_map(
        on_device, mesh=mesh, in_specs=in_specs, out_specs=out_specs, check_vma=False
    )
```

```python
import functools
import math

import jax
import jax.numpy as jnp
import ml_dtypes
import numpy as np
from jax import lax
from jax.experimental import pallas as pl
from jax.experimental.pallas import tpu as pltpu
from jax.sharding import PartitionSpec as P

F32 = jnp.float32
BF16 = jnp.bfloat16
MESH = pl.DeviceIdType.MESH
N = 8
viscosity = 0.05
time_step = 0.01
drag_strength = 20.0
heating = 40.0
buoyancy = 10.0
helmholtz_shift = 0.001
local_shift = 0.5
coarse_shift = 0.02
gll_points = (
    -1.0,
    -0.8717401485096066,
    -0.5917001814331423,
    -0.2092992179024789,
    0.2092992179024789,
    0.5917001814331423,
    0.8717401485096066,
    1.0,
)


def legendre_seven(points):
    squared = points * points
    return points * (((429.0 * squared - 693.0) * squared + 315.0) * squared - 35.0) / 16.0


def jacobi_eigen(matrix):
    current = np.array(matrix)
    basis = np.eye(8)
    for rounds in range(12):
        for first in range(7):
            for second in range(first + 1, 8):
                rotation_angle = 0.5 * math.atan2(
                    2.0 * float(current[first, second]),
                    float(current[second, second] - current[first, first]),
                )
                cosine = math.cos(rotation_angle)
                sine = math.sin(rotation_angle)
                rotation = np.eye(8)
                rotation[first, first] = cosine
                rotation[second, second] = cosine
                rotation[first, second] = sine
                rotation[second, first] = -sine
                current = rotation.T @ current @ rotation
                basis = basis @ rotation
    return (np.sum(current * np.eye(8), axis=0), basis)


def gll_tables():
    gll_nodes = np.array(gll_points)
    values = legendre_seven(gll_nodes)
    weights = 2.0 / (56.0 * values * values)
    differ = gll_nodes[:, None] - gll_nodes[None, :] + np.eye(8)
    derivative = values[:, None] / values[None, :] / differ * (1.0 - np.eye(8))
    derivative = (
        derivative + np.eye(8) * np.array([-14.0, 0.0, 0.0, 0.0, 0.0, 0.0, 0.0, 14.0])[None, :]
    )
    stiffness = derivative.T @ (weights[:, None] * derivative)
    scaled = stiffness / np.sqrt(np.outer(weights, weights))
    scaled = 0.5 * (scaled + scaled.T)
    eigen_values, eigen_vectors = jacobi_eigen(scaled)
    eigen_basis = eigen_vectors / np.sqrt(weights)[:, None]
    return (gll_nodes, weights, derivative, eigen_basis, np.maximum(eigen_values, 0.0))


def hartley_tables(count):
    index = np.arange(count)
    angle = 2.0 * np.pi / count * (index[:, None] * index[None, :] % count)
    hartley = (np.cos(angle) + np.sin(angle)) / np.sqrt(count)
    return hartley, 2.0 - 2.0 * np.cos(2.0 * np.pi / count * index)


def cosine_tables(count):
    index = np.arange(count)
    angle = np.pi / count * (index[:, None] + 0.5) * index[None, :]
    norms = np.where(index == 0, np.sqrt(1.0 / count), np.sqrt(2.0 / count))
    return np.cos(angle) * norms[None, :], 2.0 - 2.0 * np.cos(np.pi / count * index)


def thirds(matrix):
    pieces = []
    for piece in range(3):
        pieces.append(matrix.astype(np.float32).astype(ml_dtypes.bfloat16))
        matrix = matrix - pieces[-1].astype(np.float64)
    return pieces


def mode_pieces(modes):
    return modes // 128 if modes > 128 and modes % 128 == 0 else 1


DX, DY, KXY = range(3)
ZD, ZK, ZRESTRICT = range(3)
FORWARD, BACK = range(2)
ZFORWARD, ZBACK, ZPROLONG = range(3)
MASS, WXY, WZ, STEP, INVERSE, COPIES, SPECTRUM, CORNERS, SIDES = range(9)


@functools.lru_cache(maxsize=None)
def constants(parts_x, parts_y, height):
    nodes, weights, derivative, basis, values = gll_tables()
    layers = height // N
    levels = layers + 1
    group = height // 4
    assert levels + 2 <= group
    eye = np.eye(N)
    diagonal = np.diag(weights)
    stiffness = derivative.T @ diagonal @ derivative

    lefts = np.concatenate(
        [
            np.kron(derivative, eye),
            np.kron(eye, derivative),
            np.kron(stiffness, diagonal) + np.kron(diagonal, stiffness),
        ],
        axis=0,
    )
    high, low, rest = thirds(lefts)
    left_exact = np.concatenate([high, high, low, low, rest], axis=1)
    high, low, rest = thirds(np.concatenate([np.kron(basis.T, basis.T), np.kron(basis, basis)]))
    left_table = np.concatenate([high, high, low, low], axis=1)

    near, far = (1.0 - nodes) / 2.0, (1.0 + nodes) / 2.0
    vertical = np.zeros((height, levels))
    for layer in range(layers):
        vertical[layer * N : layer * N + N, layer] = near
        vertical[layer * N : layer * N + N, layer + 1] = far
    cosine, eigen_z = cosine_tables(levels)
    prolong_z = vertical @ cosine
    place = np.arange(height)
    face = np.where((np.arange(N) == 0) | (np.arange(N) == N - 1), 2.0, 1.0)
    count_z = np.where((place == 0) | (place == height - 1), 1.0, np.tile(face, layers))
    grouped = np.zeros((height, 4, group))
    grouped[:, :, :levels] = prolong_z[:, None, :]
    grouped = grouped.reshape(height, height)
    many = np.eye(layers)
    rights = [np.kron(many, derivative.T), np.kron(many, stiffness)]
    high, low, rest = thirds(np.concatenate(rights, axis=1))
    right_exact = np.concatenate([high, high, low, low, rest], axis=0)
    high, low, rest = thirds(grouped)
    right_exact = np.concatenate(
        [right_exact, np.concatenate([high, high, low, low, high], axis=0)], axis=1
    )
    rights = [np.kron(many, basis), np.kron(many, basis.T), grouped.T]
    high, low, rest = thirds(np.concatenate(rights, axis=1))
    right_table = np.concatenate([high, high, low], axis=0)

    weight_xy = np.kron(weights, weights)[:, None] * np.ones((1, height))
    weight_z = np.ones((N * N, 1)) * np.tile(weights, layers)[None, :]
    mass = weight_xy * weight_z
    count_xy = np.kron(face, face)
    copies = count_xy[:, None] * count_z[None, :]
    spectrum = (values[:, None] + values[None, :]).reshape(-1)[:, None] + np.tile(values, layers)
    near_x, far_x = np.repeat(near, N), np.repeat(far, N)
    near_y, far_y = np.tile(near, N), np.tile(far, N)
    sides = np.zeros((N * N, height))
    sides[:, 0], sides[:, 1], sides[:, 2], sides[:, 3] = near_x, far_x, near_y, far_y
    corner = np.stack([near_x * near_y, near_x * far_y, far_x * near_y, far_x * far_y], axis=1)
    corners = np.repeat(corner, group, axis=1)
    plain = np.concatenate(
        [
            mass,
            weight_xy,
            weight_z,
            time_step / (mass * copies),
            1.0 / (mass * copies),
            1.0 / copies,
            1.0 / (spectrum + local_shift),
            corners,
            sides,
        ],
        axis=0,
    ).astype(np.float32)

    hartley_x, eigen_x = hartley_tables(parts_x)
    hartley_y, eigen_y = hartley_tables(parts_y)
    vertex = []
    for step_x in (0, 1):
        for step_y in (0, 1):
            vertex.append(
                np.kron(np.roll(hartley_x, -step_x, axis=1), np.roll(hartley_y, -step_y, axis=1))
            )
    modes = parts_x * parts_y
    pieces = mode_pieces(modes)
    high, low, rest = thirds(np.stack(vertex))
    vertex_table = np.stack([high, low]).reshape(8, pieces, modes // pieces, modes)
    vertex_table = vertex_table.transpose(1, 0, 2, 3).reshape(pieces, -1, modes)
    rows = np.concatenate(
        [np.repeat(hartley_x, parts_y, axis=1), np.tile(hartley_y, (1, parts_x))], axis=0
    ).astype(np.float32)
    rows = rows.reshape(parts_x + parts_y, pieces, -1).transpose(1, 0, 2)
    horizontal = (eigen_x[:, None] + eigen_y[None, :]).reshape(-1)
    inverse = np.zeros((modes, 4, group))
    inverse[:, :, :levels] = (
        1.0 / (2.0 * (horizontal[:, None] + eigen_z[None, :]) + coarse_shift)
    )[:, None, :]
    inverse = inverse.reshape(pieces, -1, height).astype(np.float32)
    return left_exact, right_exact, left_table, right_table, plain, vertex_table, rows, inverse


def split(values):
    high = values.astype(BF16)
    return high, (values - high.astype(F32)).astype(BF16)


def split_thrice(values):
    high = values.astype(BF16)
    rest = values - high.astype(F32)
    low = rest.astype(BF16)
    return high, low, (rest - low.astype(F32)).astype(BF16)


def product(first, second):
    return jnp.dot(first, second, preferred_element_type=F32)


EXCHANGES = (4, 4, 1, 1, 1, 6)
GATHERS = 3
OPERANDS = 11


def kernel(
    parts,
    *refs,
):
    operands, (state_ref, pressure_ref) = refs[:OPERANDS], refs[OPERANDS : OPERANDS + 2]
    held = refs[OPERANDS + 2 : 2 * OPERANDS + 2]
    load_sem, *scratch = refs[2 * OPERANDS + 2 :]
    loads = [
        pltpu.make_async_copy(source, here, load_sem.at[index])
        for index, (source, here) in enumerate(zip(operands, held))
    ]
    for load in loads:
        load.start()
    (
        flow_ref,
        left_exact_ref,
        right_exact_ref,
        plain_ref,
        roof_ref,
        old_ref,
        rows_ref,
        left_ref,
        right_ref,
        vertex_ref,
        modes_ref,
    ) = held

    parts_x, parts_y = parts
    devices = parts_x * parts_y
    count = len(EXCHANGES)
    fields = scratch[0:count]
    y_out = scratch[count : 2 * count]
    c_out = scratch[2 * count : 3 * count]
    x_in = scratch[3 * count : 4 * count]
    y_in = scratch[4 * count : 5 * count]
    c_in = scratch[5 * count : 6 * count]
    row_out, gathered, send_sem, recv_sem, row_send, row_recv = scratch[6 * count :]
    height = old_ref.shape[1]
    points = old_ref.shape[0]

    my_x, my_y = lax.axis_index("gx"), lax.axis_index("gy")
    me = my_x * parts_y + my_y

    barrier = pltpu.get_barrier_semaphore()

    def each_other(action):
        if devices <= 64:
            all_x = [lax.rem(my_x + step, parts_x) for step in range(parts_x)]
            all_y = [lax.rem(my_y + step, parts_y) for step in range(parts_y)]
            for step in range(1, devices):
                action(all_x[step // parts_y], all_y[step % parts_y])
            return

        def one(step, carry):
            other = lax.rem(me + step, devices)
            action(other // parts_y, lax.rem(other, parts_y))
            return carry

        lax.fori_loop(1, devices, one, 0)

    def greet(other_x, other_y):
        pl.semaphore_signal(barrier, inc=1, device_id=(other_x, other_y), device_id_type=MESH)

    each_other(greet)

    before_x, after_x = lax.rem(my_x + parts_x - 1, parts_x), lax.rem(my_x + 1, parts_x)
    before_y, after_y = lax.rem(my_y + parts_y - 1, parts_y), lax.rem(my_y + 1, parts_y)

    def block(which):
        return plain_ref[which * points : (which + 1) * points, :]

    def left_exact(values, first, last):
        high, low = split(values)
        stacked = jnp.concatenate([high, low, high, low, high], axis=0)
        return product(left_exact_ref[first * points : last * points, :], stacked)

    def right_exact(values, first, last):
        high, low = split(values)
        stacked = jnp.concatenate([high, low, high, low, high], axis=1)
        return product(stacked, right_exact_ref[:, first * height : last * height])

    def left(values, first, last):
        high, low = split(values)
        stacked = jnp.concatenate([high, low, high, low], axis=0)
        return product(left_ref[first * points : last * points, :], stacked)

    def right(values, first, last):
        high, low = split(values)
        stacked = jnp.concatenate([high, low, high], axis=1)
        return product(stacked, right_ref[:, first * height : last * height])

    lane = lax.broadcasted_iota(jnp.int32, (points, height), 1)
    joins_up = ((lane & (N - 1)) == N - 1) & (lane < height - 1)
    joins_down = ((lane & (N - 1)) == 0) & (lane > 0)

    def pair_z(values):
        up = pltpu.roll(values, height - 1, 1)
        down = pltpu.roll(values, 1, 1)
        return values + jnp.where(joins_up, up, jnp.where(joins_down, down, 0.0))

    def copies(which):
        field = fields[which]
        plan = []
        for corner, target in enumerate(
            ((after_x, after_y), (after_x, before_y), (before_x, after_y), (before_x, before_y))
        ):
            plan.append((c_out[which].at[corner], c_in[which].at[corner], target))
        x_faces = (field.at[:, points - N : points, :], field.at[:, 0:N, :])
        for side, target in ((0, after_x), (1, before_x)):
            plan.append((x_faces[side], x_in[which].at[side], (target, my_y)))
        for side, target in ((0, after_y), (1, before_y)):
            plan.append((y_out[which].at[side], y_in[which].at[side], (my_x, target)))
        return [
            pltpu.make_async_remote_copy(
                src_ref=source,
                dst_ref=landing,
                send_sem=send_sem.at[which, index],
                recv_sem=recv_sem.at[which, index],
                device_id=target,
                device_id_type=MESH,
            )
            for index, (source, landing, target) in enumerate(plan)
        ]

    def stage(which, values, first=0):
        values = [pair_z(value) for value in values]
        for index, value in enumerate(values, first):
            fields[which][index] = value
            solid = value.reshape(N, N, height)
            y_out[which][0, index * N : index * N + N, :] = solid[:, N - 1, :]
            y_out[which][1, index * N : index * N + N, :] = solid[:, 0, :]
            for corner, row in enumerate((points - 1, points - N, N - 1, 0)):
                c_out[which][corner, index : index + 1, :] = value[row : row + 1, :]
        return values

    def start(which, values):
        values = stage(which, values)
        for copy in copies(which):
            copy.start()
        return values

    row_of_x = lax.broadcasted_iota(jnp.int32, (N, height), 0)

    def finish(which, values):
        for copy in copies(which):
            copy.wait_recv()
        return join(which, values)

    def join(which, values, first=0):
        results = []
        for index, value in enumerate(values, first):
            solid = value.reshape(N, N, height)
            from_x = x_in[which][:, index]
            first_y = y_in[which][0, index * N : index * N + N, :]
            last_y = y_in[which][1, index * N : index * N + N, :]
            corner = [c_in[which][which_one, index : index + 1, :] for which_one in range(4)]
            first_y = first_y + jnp.where(row_of_x == 0, corner[0], 0.0)
            last_y = last_y + jnp.where(row_of_x == 0, corner[1], 0.0)
            first_y = first_y + jnp.where(row_of_x == N - 1, corner[2], 0.0)
            last_y = last_y + jnp.where(row_of_x == N - 1, corner[3], 0.0)
            slabs = []
            for x in range(N):
                slab = solid[x]
                if x == 0:
                    slab = slab + from_x[0]
                if x == N - 1:
                    slab = slab + from_x[1]
                slab = slab + jnp.where(row_of_x == 0, first_y[x : x + 1, :], 0.0)
                slab = slab + jnp.where(row_of_x == N - 1, last_y[x : x + 1, :], 0.0)
                slabs.append(slab)
            results.append(jnp.concatenate(slabs, axis=0))
        return results

    def spread(which, row):
        row_out[which] = row
        gathered[which, pl.ds(me, 1), :] = row

        def send(other_x, other_y):
            pltpu.make_async_remote_copy(
                src_ref=row_out.at[which],
                dst_ref=gathered.at[which, pl.ds(me, 1), :],
                send_sem=row_send.at[which],
                recv_sem=row_recv.at[which],
                device_id=(other_x, other_y),
                device_id_type=MESH,
            ).start()

        each_other(send)

    def all_rows(which):
        return pltpu.make_async_remote_copy(
            src_ref=gathered.at[which, pl.ds(0, devices - 1), :],
            dst_ref=gathered.at[which, pl.ds(0, devices - 1), :],
            send_sem=row_send.at[which],
            recv_sem=row_recv.at[which],
            device_id=(after_x, my_y),
            device_id_type=MESH,
        )

    def collect(which):
        all_rows(which).wait_recv()
        return gathered[which]

    one_row = lax.broadcasted_iota(jnp.int32, (1, height), 1)
    group = height // 4
    spare = height // N + 1

    def operate(values):
        image = left_exact(values, KXY, KXY + 1) * weight_z
        image = image + weight_xy * right_exact(values, ZK, ZK + 1)
        return image + helmholtz_shift * mass * values

    def gradient(values):
        xy = left_exact(values, DX, DY + 1)
        z = right_exact(values, ZD, ZD + 1)
        return [mass * xy[:points], mass * xy[points:], mass * z]

    def coarse_row(part):
        high, low, rest = split_thrice(part)
        stacked = jnp.concatenate([high, low, high, low, rest], axis=1)
        table = right_exact_ref[:, ZRESTRICT * height : (ZRESTRICT + 1) * height]
        terms = block(CORNERS) * product(stacked, table)
        return jnp.sum(terms, axis=0, keepdims=True)

    def with_scalars(row, residual, smoothed, image):
        gamma = jnp.sum(residual * smoothed * block(COPIES), axis=0, keepdims=True)
        delta = jnp.sum(smoothed * image, axis=0, keepdims=True)
        gamma = jnp.sum(gamma, axis=1, keepdims=True)
        delta = jnp.sum(delta, axis=1, keepdims=True)
        return jnp.where(one_row == spare, gamma, jnp.where(one_row == spare + 1, delta, row))

    def scalars(rows):
        total = jnp.sum(rows, axis=0, keepdims=True)
        return total[:, spare : spare + 1], total[:, spare + 1 : spare + 2]

    def local_solve(residual):
        modal = right(left(residual, FORWARD, FORWARD + 1), ZFORWARD, ZFORWARD + 1)
        modal = modal * block(SPECTRUM)
        return left(right(modal, ZBACK, ZBACK + 1), BACK, BACK + 1)

    def own_modes(piece):
        sides = block(SIDES)
        next_x, next_y = lax.rem(my_x + 1, parts_x), lax.rem(my_y + 1, parts_y)

        def row(which):
            return rows_ref[piece, pl.ds(which, 1), :]

        own_x = sides[:, 0:1] * row(my_x) + sides[:, 1:2] * row(next_x)
        own_y = sides[:, 2:3] * row(parts_x + my_y) + sides[:, 3:4] * row(parts_x + next_y)
        return split(own_x * own_y)

    pieces = modes_ref.shape[0]
    length = modes_ref.shape[1]
    span = length if pieces == 1 else 2 * length
    mode_lane = lax.broadcasted_iota(jnp.int32, (length, height), 1)

    def coarse_piece(piece, stacked, own):
        each = product(vertex_ref[piece, :, :span], stacked[:span])
        for begin in range(span, devices, span):
            lines = slice(begin, begin + span)
            each = each + product(vertex_ref[piece, :, lines], stacked[lines])
        tops, lows = each[: 4 * length], each[4 * length :]
        each = (tops[:, 2 * height :] + lows[:, height : 2 * height]) + (
            tops[:, height : 2 * height] + lows[:, :height]
        )
        each = each + tops[:, :height]
        total = jnp.zeros((length, height), F32)
        for corner in range(4):
            chosen = (mode_lane >= corner * group) & (mode_lane < corner * group + group)
            total = jnp.where(chosen, each[corner * length : (corner + 1) * length], total)
        levels = right(total * modes_ref[piece], ZPROLONG, ZPROLONG + 1)
        high, low = split(levels)
        own_high, own_low = own
        return product(own_high, high) + (product(own_high, low) + product(own_low, high))

    def coarse_solve(rows):
        stacked = jnp.concatenate(split_thrice(rows), axis=1)
        if pieces == 1:
            return coarse_piece(0, stacked, own)
        total = jnp.zeros((points, height), F32)
        for piece in range(pieces):
            total = total + coarse_piece(piece, stacked, own_modes(piece))
        return total

    for load in loads[:5]:
        load.wait()
    mass, weight_xy, weight_z = block(MASS), block(WXY), block(WZ)
    flow = [flow_ref[part * points : (part + 1) * points, :] for part in range(4)]
    u, v, w, theta = flow
    xy = left_exact(jnp.concatenate(flow, axis=1), DX, KXY + 1)
    z = right_exact(flow_ref[...], ZD, ZK + 1)
    canopy = jnp.where(lane < N * roof_ref[...], 1.0, 0.0)
    drag = drag_strength * canopy * jnp.sqrt(u * u + v * v + w * w)
    forcing = [-drag * u, -drag * v, -drag * w + buoyancy * theta, heating * canopy]
    rates = []
    for part in range(4):
        lanes = slice(part * height, (part + 1) * height)
        rows = slice(part * points, (part + 1) * points)
        advection = u * xy[:points, lanes] + v * xy[points : 2 * points, lanes] + w * z[rows, :height]
        friction = xy[2 * points :, lanes] * weight_z + weight_xy * z[rows, height:]
        rates.append(mass * (forcing[part] - advection) - viscosity * friction)
    pl.semaphore_wait(barrier, devices - 1)
    rates = start(0, rates)

    for load in loads[5:]:
        load.wait()
    old = old_ref[...]
    old_image = operate(old)
    old_gradient = stage(1, gradient(old), 1)
    own = own_modes(0) if pieces == 1 else None

    rates = finish(0, rates)
    step = block(STEP)
    provisional = [values + step * rate for values, rate in zip(flow, rates)]
    provisional[2] = jnp.where((lane == 0) | (lane == height - 1), 0.0, provisional[2])
    divergence = (
        left_exact(provisional[0], DX, DX + 1)
        + left_exact(provisional[1], DY, DY + 1)
        + right_exact(provisional[2], ZD, ZD + 1)
    )
    raw = -mass * divergence - old_image
    whole = start(1, [raw])
    spread(0, coarse_row(raw))
    residual = finish(1, whole)[0]

    local = start(2, [local_solve(residual)])
    coarse = coarse_solve(collect(0))
    first = finish(2, local)[0] + coarse
    raw = operate(first)
    image = start(3, [raw])
    spread(1, with_scalars(coarse_row(raw), residual, first, raw))
    image = finish(3, image)[0]

    local = start(4, [local_solve(image)])
    first_gradient = stage(5, gradient(first))
    rows = collect(1)
    coarse = coarse_solve(rows)
    gamma_first, delta_first = scalars(rows)
    alpha_first = gamma_first / delta_first
    residual = residual - alpha_first * image
    second = first - alpha_first * (finish(4, local)[0] + coarse)
    raw, second_gradient = operate(second), gradient(second)
    spread(2, with_scalars(jnp.zeros((1, height), F32), residual, second, raw))
    second_gradient = stage(5, second_gradient, 3)
    for copy in copies(5):
        copy.start()
    gradients = join(1, old_gradient, 1)
    gamma, delta = scalars(collect(2))
    ratio = gamma / gamma_first
    alpha = gamma / (delta - ratio * gamma / alpha_first)
    weight_first = alpha_first + alpha * ratio
    pressure_ref[...] = old + weight_first * first + alpha * second
    state_ref[3 * points : 4 * points, :] = provisional[3]
    gradients += finish(5, first_gradient)
    second_gradient = join(5, second_gradient, 3)
    inverse = block(INVERSE)
    for part in range(3):
        total = gradients[part] + weight_first * gradients[3 + part] + alpha * second_gradient[part]
        state_ref[part * points : (part + 1) * points, :] = provisional[part] - total * inverse

    for which in range(count):
        for copy in copies(which):
            copy.wait_send()
    for which in range(GATHERS):
        all_rows(which).wait_send()


def on_device(flow_state, building_height, pressure_old):
    parts = (lax.axis_size("gx"), lax.axis_size("gy"))
    devices = parts[0] * parts[1]
    components, width, depth, height = flow_state.shape
    points = width * depth
    assert width == N and depth == N and components == 4
    tables = constants(parts[0], parts[1], height)
    left_exact, right_exact, left, right, plain, vertex, rows, modes = [
        jnp.asarray(table) for table in tables
    ]
    operands = [
        flow_state.reshape(components * points, height),
        left_exact,
        right_exact,
        plain,
        building_height,
        pressure_old.reshape(points, height),
        rows,
        left,
        right,
        vertex,
        modes,
    ]
    scratch = [pltpu.VMEM(operand.shape, operand.dtype) for operand in operands]
    scratch += [pltpu.SemaphoreType.DMA((len(operands),))]
    scratch += [pltpu.VMEM((number, points, height), F32) for number in EXCHANGES]
    scratch += [pltpu.VMEM((2, number * N, height), F32) for number in EXCHANGES]
    scratch += [pltpu.VMEM((4, number, height), F32) for number in EXCHANGES]
    scratch += [pltpu.VMEM((2, number, N, height), F32) for number in EXCHANGES]
    scratch += [pltpu.VMEM((2, number * N, height), F32) for number in EXCHANGES]
    scratch += [pltpu.VMEM((4, number, height), F32) for number in EXCHANGES]
    scratch += [
        pltpu.VMEM((GATHERS, 1, height), F32),
        pltpu.VMEM((GATHERS, devices, height), F32),
        pltpu.SemaphoreType.DMA((len(EXCHANGES), 8)),
        pltpu.SemaphoreType.DMA((len(EXCHANGES), 8)),
        pltpu.SemaphoreType.DMA((GATHERS,)),
        pltpu.SemaphoreType.DMA((GATHERS,)),
    ]
    whole = pl.BlockSpec(memory_space=pltpu.VMEM)
    state, pressure = pl.pallas_call(
        functools.partial(kernel, parts),
        out_shape=(
            pltpu.VMEM((components * points, height), F32),
            pltpu.VMEM((points, height), F32),
        ),
        in_specs=[pl.BlockSpec(memory_space=pltpu.HBM)] * len(operands),
        out_specs=(whole, whole),
        scratch_shapes=scratch,
        compiler_params=pltpu.CompilerParams(
            collective_id=0, has_side_effects=True, vmem_limit_bytes=60 * 2**20
        ),
    )(*operands)
    return state.reshape(flow_state.shape), pressure.reshape(pressure_old.shape)


def solution(mesh):
    in_specs = (P(None, "gx", "gy", None), P("gx", "gy"), P("gx", "gy", None))
    out_specs = (P(None, "gx", "gy", None), P("gx", "gy", None))
    return jax.shard_map(
        on_device, mesh=mesh, in_specs=in_specs, out_specs=out_specs, check_vma=False
    )
```
